32 devices in a mesh: grp: 2 (over x), gx: 8 (over z, y), gy: 2 (over core).
Axes of the slice: x: 2, y: 2, z: 4, core: 2. Of those that a mesh axis runs over, the one named last changes fastest.
Arguments:
- fields: float32 [4, 4, 48, 512, 512], P('grp', None, None, 'gx', 'gy'), parts along dimension 0, may hold values from -2.5 to 2.5
- member_index: int32 [4], P('grp'), parts along dimension 0, may hold values from 0 to 7
- member_table: float32 [8, 4, 4], replicated, may hold values from 0.5 to 2
- seed_x: int32 [4, 16], P('grp'), parts along dimension 0, may hold values from 0 to 511
- seed_y: int32 [4, 16], P('grp'), parts along dimension 0, may hold values from 0 to 511
- seed_z: int32 [4, 16], P('grp'), parts along dimension 0, may hold values from 0 to 47
- start_basis: float32 [4, 512, 64], P('grp'), parts along dimension 0, may hold values from -6 to 6
Outputs:
- fields_next: float32 [4, 4, 48, 512, 512], P('grp', None, None, 'gx', 'gy'), parts along dimension 0
- basis: float32 [4, 512, 64], P('grp'), parts along dimension 0
- core: float32 [4, 64, 4, 4, 512], P('grp', 'gx', None, None, 'gy'), parts along dimension 0
The draws below stay inside these ranges and needn't reach their ends.
There are 2 independent parts, one for each index of `grp`. The reference program is written for one: setup_inputs(seed, part) draws one part's arguments, and reference() takes and returns one part's arrays. A program takes and returns all parts, laid end to end along the dimension named above; an argument that names none is the same for every part. Nothing has to cross between parts.
All inputs are finite; a program needn't handle non-finite values.
Results may differ from the reference program's by a relative error of at most 0.0003.
Values sent between devices are 32-bit elements; how exact they have to be, the bound alone decides.
No kernel may reach another device: no remote copies, remote signals or barrier semaphores. Data moves between devices by JAX's collectives and lax.ppermute only.
A program may use at most 448 MiB of HBM per device.

```python
import math
import jax
import jax.numpy as jnp
from jax import lax

M = 2
F = 4
NX = 512
NY = 512
ZW = 48
ZS = 4
R = 64
ITERS = 3
NSEED = 16
P_SIZE = 8


def place_ends(entries, rng, least, high):
    dims = entries.shape
    spot = [jax.random.randint(jax.random.fold_in(rng, axis), (), 0, dims[axis]) for axis in range(len(dims))]
    entries = entries.at[tuple(spot)].set(least)
    longest = dims.index(max(dims))
    spot[longest] = (spot[longest] + 1) % dims[longest]
    return entries.at[tuple(spot)].set(high)


def levels(stream_key, dims, pieces, least, high):
    loudness = 1.0
    for dim, blocks in pieces:
        steps = jax.random.uniform(jax.random.fold_in(jax.random.fold_in(stream_key, 6), dim), (blocks,), jnp.float32, least / len(pieces), high / len(pieces))
        loudness = loudness * jnp.repeat(jnp.exp(steps), dims[dim] // blocks).reshape((-1,) + (1,) * (len(dims) - 1 - dim))
    return loudness


def noise(own_key, extent, deviation, limit, shards=(), kind=jnp.bfloat16):
    values = deviation * jax.random.normal(own_key, extent, jnp.float32)
    if shards:
        values = values * levels(own_key, extent, shards, -0.22, 0.18)
    return jnp.clip(values, -limit, limit).astype(kind)


def setup_inputs(seed: int = 0, part: int = 0) -> dict:
    splits = jax.random.split(jax.random.key(seed), 8)
    part_keys = jax.random.split(jax.random.fold_in(splits[7], part), 8)
    return {
        "fields": noise(part_keys[0], (M, F, ZW, NX, NY), 0.5, 2.5, ((3, 8), (4, 2)), jnp.float32),
        "member_index": jax.random.randint(part_keys[1], (M,), 0, P_SIZE).astype(jnp.int32),
        "member_table": jnp.clip(jnp.exp(jax.random.uniform(splits[2], (P_SIZE, F, 4), jnp.float32, math.log(0.5), math.log(2.0))), 0.5, 2.0),
        "seed_x": place_ends(jax.random.randint(part_keys[3], (M, NSEED), 0, NX), jax.random.fold_in(part_keys[3], 1), 0, NX - 1).astype(jnp.int32),
        "seed_y": place_ends(jax.random.randint(part_keys[4], (M, NSEED), 0, NY), jax.random.fold_in(part_keys[4], 1), 0, NY - 1).astype(jnp.int32),
        "seed_z": place_ends(jax.random.randint(part_keys[5], (M, NSEED), 0, ZW), jax.random.fold_in(part_keys[5], 1), 0, ZW - 1).astype(jnp.int32),
        "start_basis": noise(part_keys[6], (M, NX, R), 1.0, 6.0, (), jnp.float32),
    }


highest = lax.Precision.HIGHEST
time_step = 0.05
bump_width = 18.0
source_gain = 0.5

def member_params(member_index, member_table):
    table_rows = member_table.shape[0]
    onehot = (member_index[:, None] == jnp.arange(table_rows, dtype=jnp.int32)[None, :]).astype(jnp.float32)
    return jnp.einsum('mp,pfk->mfk', onehot, member_table, precision=highest)

def seed_bumps(seed_x, seed_y, seed_z, x_start, y_start, rows_x, rows_y, planes):
    along_x = (x_start + jnp.arange(rows_x, dtype=jnp.int32)).astype(jnp.float32)
    along_y = (y_start + jnp.arange(rows_y, dtype=jnp.int32)).astype(jnp.float32)
    along_z = jnp.arange(planes, dtype=jnp.int32).astype(jnp.float32)
    bump_x = jnp.exp(-jnp.square(along_x[None, None, :] - seed_x[:, :, None].astype(jnp.float32)) / bump_width)
    bump_y = jnp.exp(-jnp.square(along_y[None, None, :] - seed_y[:, :, None].astype(jnp.float32)) / bump_width)
    bump_z = jnp.exp(-jnp.square(along_z[None, None, :] - seed_z[:, :, None].astype(jnp.float32)) / bump_width)
    plane_x = bump_z[:, :, :, None] * bump_x[:, :, None, :]
    return jnp.einsum('mszx,msy->mzxy', plane_x, bump_y, precision=highest)

def advance(fields, padded, params, source):
    lap_plane = padded[..., 2:, 1:-1] + padded[..., :-2, 1:-1] + padded[..., 1:-1, 2:] + padded[..., 1:-1, :-2]
    above = jnp.concatenate([fields[:, :, 1:], fields[:, :, -1:]], axis=2)
    below = jnp.concatenate([fields[:, :, :1], fields[:, :, :-1]], axis=2)
    laplace = lap_plane + above + below - 6.0 * fields
    kappa = params[:, :, 0][:, :, None, None, None]
    mobility = params[:, :, 1][:, :, None, None, None]
    gamma = params[:, :, 2][:, :, None, None, None]
    strength = params[:, :, 3][:, :, None, None, None]
    squares = jnp.sum(fields * fields, axis=1, keepdims=True)
    drive = fields * fields * fields - fields + gamma * fields * (squares - fields * fields)
    return fields + time_step * mobility * (kappa * laplace - drive) + source_gain * strength * source[:, None]

def orthonormal(image):
    cov = jnp.einsum('mxk,mxl->mkl', image, image, precision=highest)
    lower = jnp.linalg.cholesky(cov)
    return lax.linalg.triangular_solve(lower, image, left_side=False, lower=True, transpose_a=True)

def reference(fields, member_index, member_table, seed_x, seed_y, seed_z, start_basis):
    padded = jnp.pad(fields, ((0, 0), (0, 0), (0, 0), (1, 1), (1, 1)))
    params = member_params(member_index, member_table)
    source = seed_bumps(seed_x, seed_y, seed_z, 0, 0, NX, NY, ZW)
    fields_next = advance(fields, padded, params, source)
    slab = fields_next[:, :, :ZS]
    gram = jnp.einsum('mfzxy,mfzwy->mxw', slab, slab, precision=highest)
    basis = start_basis
    for turn in range(ITERS):
        basis = orthonormal(jnp.einsum('mxw,mwk->mxk', gram, basis, precision=highest))
    core = jnp.einsum('mxr,mfzxy->mrfzy', basis, slab, precision=highest)
    return (fields_next, basis, core)
```

```python
import functools
import jax
import jax.numpy as jnp
from jax import lax
from jax.experimental import pallas as pl
from jax.experimental.pallas import tpu as pltpu
from jax.sharding import PartitionSpec as P

ZS = 4
ITERS = 3
ZB = 8

highest = lax.Precision.HIGHEST
time_step = 0.05
bump_width = 18.0
source_gain = 0.5
f32 = jnp.float32
bf16 = jnp.bfloat16
MIB = 1 << 20


def smem():
    return pl.BlockSpec(memory_space=pltpu.SMEM)


def vmem():
    return pl.BlockSpec(memory_space=pltpu.VMEM)


def params_of(limit):
    return pltpu.CompilerParams(vmem_limit_bytes=limit * MIB)


def split3(value):
    high = value.astype(bf16)
    rest = value - high.astype(f32)
    middle = rest.astype(bf16)
    low = (rest - middle.astype(f32)).astype(bf16)
    return high, middle, low


def edges_kernel(idx_ref, first_ref, last_ref, half_ref, top_ref, bottom_ref, side_ref):
    fb, planes, rows = half_ref.shape[1:4]
    lane = lax.broadcasted_iota(jnp.int32, (rows, 128), 1)
    offset = jnp.where(idx_ref[1] == 0, 1, 0)
    for f in range(fb):
        side = jnp.zeros((rows, 128), f32)
        for z in range(planes):
            top_ref[0, f, z : z + 1, :] = first_ref[0, f, z, 0:1, :]
            bottom_ref[0, f, z : z + 1, :] = last_ref[0, f, z, 7:8, :]
            turned = pltpu.roll(half_ref[0, f, z], z + offset, 1)
            side = jnp.where(lane == z, turned, side)
        side_ref[0, f] = side


def edges(idx, fields, planes, fb):
    m, f, _, rows, cols = fields.shape
    last = rows // 8 - 1
    tail = cols // 128 - 1
    edge_row = jax.ShapeDtypeStruct((m, f, planes, cols), f32)
    return pl.pallas_call(
        edges_kernel,
        grid_spec=pltpu.PrefetchScalarGridSpec(
            num_scalar_prefetch=1,
            grid=(m, f // fb),
            in_specs=[
                pl.BlockSpec((1, fb, planes, 8, cols), lambda i, j, s: (i, j, 0, 0, 0)),
                pl.BlockSpec((1, fb, planes, 8, cols), lambda i, j, s: (i, j, 0, last, 0)),
                pl.BlockSpec(
                    (1, fb, planes, rows, 128),
                    lambda i, j, s: (i, j, 0, 0, jnp.where(s[1] == 0, tail, 0)),
                ),
            ],
            out_specs=[
                pl.BlockSpec((1, fb, planes, cols), lambda i, j, s: (i, j, 0, 0)),
                pl.BlockSpec((1, fb, planes, cols), lambda i, j, s: (i, j, 0, 0)),
                pl.BlockSpec((1, fb, rows, 128), lambda i, j, s: (i, j, 0, 0)),
            ],
        ),
        out_shape=[edge_row, edge_row, jax.ShapeDtypeStruct((m, f, rows, 128), f32)],
        compiler_params=params_of(32),
        cost_estimate=pl.CostEstimate(
            flops=m * f * planes * rows * 256,
            bytes_accessed=m * f * planes * (rows * 128 + 16 * cols) * 4,
            transcendentals=0,
        ),
    )(idx, fields, fields, fields)


def step_block(idx_ref, coef_ref, refs, zb, z0, m, store):
    now, before, after, xu, xd, yh, sx, sy, sz = refs
    nf, rows, cols = now.shape[1], now.shape[3], now.shape[4]
    tiles = cols // 128
    wide = sx.shape[-1]
    seeds = wide // 6
    x_start = idx_ref[0] * rows
    y_start = idx_ref[1] * cols
    along_x = (x_start + lax.broadcasted_iota(jnp.int32, (rows, wide), 0)).astype(f32)
    bump_x = jnp.exp(-jnp.square(along_x - sx[0]) / bump_width)
    along_y = (y_start + lax.broadcasted_iota(jnp.int32, (wide, cols), 1)).astype(f32)
    high, middle, low = split3(jnp.exp(-jnp.square(along_y - sy[0]) / bump_width))
    part = lax.broadcasted_iota(jnp.int32, (wide, cols), 0) // seeds
    right = jnp.where(
        part == 3,
        low.astype(f32),
        jnp.where((part == 1) | (part == 5), middle.astype(f32), high.astype(f32)),
    ).astype(bf16)
    group = lax.broadcasted_iota(jnp.int32, (rows, wide), 1) // seeds
    use_low = group == 4
    use_middle = (group == 2) | (group == 5)
    lane = lax.broadcasted_iota(jnp.int32, (8, 128), 1)
    row = lax.broadcasted_iota(jnp.int32, (8, cols), 0)
    is_left = lane == 0
    is_right = lane == 127
    is_top = row == 0
    is_bottom = row == 7
    at_end = idx_ref[1] == 0
    gain_left = jnp.where(at_end, 0.0, 1.0).astype(f32)
    gain_right = jnp.where(at_end, 1.0, 0.0).astype(f32)
    coefs = [[coef_ref[m, f, k] for k in range(5)] for f in range(nf)]

    def plane(z, below_of, above_of):
        along_z = (z0 + z).astype(f32) if not isinstance(z0 + z, int) else f32(z0 + z)
        bump_z = jnp.exp(-jnp.square(along_z - sz[0]) / bump_width)
        high, middle, low = split3(bump_x * bump_z)
        left = jnp.where(
            use_low, low.astype(f32), jnp.where(use_middle, middle.astype(f32), high.astype(f32))
        ).astype(bf16)
        source = jnp.dot(left, right, preferred_element_type=f32)
        shift = jnp.where(at_end, 127 - (z0 + z), 128 - (z0 + z))
        shift = jnp.where(shift == 128, 0, shift)
        for r in range(0, rows, 8):
            cells = [now[0, f, z, r : r + 8, :] for f in range(nf)]
            squared = [c * c for c in cells]
            squares = squared[0]
            for f in range(1, nf):
                squares = squares + squared[f]
            src = source[r : r + 8, :]
            for f in range(nf):
                c = cells[f]
                a, c0, c1, c2, s = coefs[f]
                if r == 0:
                    over = xu[0, f, pl.ds(z0 + z, 1), :]
                else:
                    over = now[0, f, z, r - 1 : r, :]
                if r + 8 == rows:
                    under = xd[0, f, pl.ds(z0 + z, 1), :]
                else:
                    under = now[0, f, z, r + 8 : r + 9, :]
                up = jnp.where(is_top, over, pltpu.roll(c, 1, 0))
                down = jnp.where(is_bottom, under, pltpu.roll(c, 7, 0))
                halo = pltpu.roll(yh[0, f, r : r + 8, :], shift, 1)
                parts = [c[:, 128 * t : 128 * t + 128] for t in range(tiles)]
                fwd = [pltpu.roll(p, 1, 1) for p in parts]
                bwd = [pltpu.roll(p, 127, 1) for p in parts]
                side = []
                for t in range(tiles):
                    from_left = halo * gain_left if t == 0 else fwd[t - 1]
                    from_right = halo * gain_right if t == tiles - 1 else bwd[t + 1]
                    side.append(
                        jnp.where(is_left, from_left, fwd[t])
                        + jnp.where(is_right, from_right, bwd[t])
                    )
                near = (
                    jnp.concatenate(side, axis=1)
                    + (up + down)
                    + (below_of(f, r) + above_of(f, r))
                )
                value = a * near + c * (c0 - c1 * squared[f] - c2 * squares) + s * src
                store(f, z, r, value)

    def prior(z):
        return lambda f, r: now[0, f, z - 1, r : r + 8, :]

    def later(z):
        return lambda f, r: now[0, f, z + 1, r : r + 8, :]

    plane(0, lambda f, r: before[0, f, 0, r : r + 8, :], later(0))

    def body(z, carry):
        plane(z, prior(z), later(z))
        return carry

    lax.fori_loop(1, zb - 1, body, 0)
    plane(zb - 1, prior(zb - 1), lambda f, r: after[0, f, 0, r : r + 8, :])


def bulk_kernel(idx_ref, coef_ref, *refs):
    out = refs[-1]
    m, t = pl.program_id(0), pl.program_id(1)

    def store(f, z, r, value):
        out[0, f, z, r : r + 8, :] = value

    step_block(idx_ref, coef_ref, refs[:-1], ZB, t * ZB, m, store)


def step_specs(fields, planes, zb, halo_planes, wide):
    m, f, nz, rows, cols = fields.shape

    def at(shape, index):
        return pl.BlockSpec(shape, index)

    return [
        at((1, f, zb, rows, cols), lambda i, t, s: (i, 0, t, 0, 0)),
        at((1, f, 1, rows, cols), lambda i, t, s: (i, 0, jnp.maximum(t * zb - 1, 0), 0, 0)),
        at((1, f, 1, rows, cols), lambda i, t, s: (i, 0, jnp.minimum(t * zb + zb, nz - 1), 0, 0)),
        at((1, f, halo_planes, cols), lambda i, t, s: (i, 0, 0, 0)),
        at((1, f, halo_planes, cols), lambda i, t, s: (i, 0, 0, 0)),
        at((1, f, rows, 128), lambda i, t, s: (i, 0, 0, 0)),
        at((1, 1, wide), lambda i, t, s: (i, 0, 0)),
        at((1, wide, 1), lambda i, t, s: (i, 0, 0)),
        at((1, 1, wide), lambda i, t, s: (i, 0, 0)),
    ]


def bulk(idx, coefs, fields, halos, seeds):
    m, f, nz, rows, cols = fields.shape
    wide = seeds[0].shape[-1]
    specs = step_specs(fields, nz, ZB, nz, wide)
    return pl.pallas_call(
        bulk_kernel,
        grid_spec=pltpu.PrefetchScalarGridSpec(
            num_scalar_prefetch=1,
            grid=(m, nz // ZB),
            in_specs=[smem()] + specs,
            out_specs=pl.BlockSpec((1, f, ZB, rows, cols), lambda i, t, s: (i, 0, t, 0, 0)),
        ),
        out_shape=jax.ShapeDtypeStruct(fields.shape, f32),
        compiler_params=params_of(40),
        cost_estimate=pl.CostEstimate(
            flops=fields.size * 30, bytes_accessed=fields.size * 10, transcendentals=0
        ),
    )(idx, coefs, fields, fields, fields, *halos, *seeds)


def slab_kernel(n, ppd, yb, idx_ref, coef_ref, *refs):
    ins, outs, scratch = refs[:9], refs[9 : 9 + n], refs[9 + n]
    m = pl.program_id(0)
    me = idx_ref[0]
    ysp = ins[0].shape[4] // yb

    def store(f, z, r, value):
        p = f * ZS + z
        for h in range(ysp):
            scratch[p * ysp + h, r : r + 8, :] = value[:, h * yb : h * yb + yb]

    step_block(idx_ref, coef_ref, ins, ZS, 0, m, store)
    for k in range(n):
        dest = me ^ k
        for j in range(ppd):
            outs[k][0, j] = scratch[dest * ppd + j]


def slab_pieces(n, fields):
    _, f, _, _, cols = fields.shape
    count = f * ZS
    ysp = max(1, n // count)
    return max(1, count // n), cols // ysp, count * ysp


def slab_step(idx, coefs, fields, halos, seeds, n):
    m, f, nz, rows, cols = fields.shape
    wide = seeds[0].shape[-1]
    ppd, yb, pieces = slab_pieces(n, fields)
    piece = jax.ShapeDtypeStruct((m, ppd, rows, yb), f32)
    specs = step_specs(fields, ZS, ZS, ZS, wide)
    return pl.pallas_call(
        functools.partial(slab_kernel, n, ppd, yb),
        grid_spec=pltpu.PrefetchScalarGridSpec(
            num_scalar_prefetch=1,
            grid=(m, 1),
            in_specs=[smem()] + specs,
            out_specs=[pl.BlockSpec((1, ppd, rows, yb), lambda i, t, s: (i, 0, 0, 0))] * n,
            scratch_shapes=[pltpu.VMEM((pieces, rows, yb), f32)],
        ),
        out_shape=[piece] * n,
        compiler_params=params_of(32),
        cost_estimate=pl.CostEstimate(
            flops=m * f * ZS * rows * cols * 30,
            bytes_accessed=m * f * ZS * rows * cols * 10,
            transcendentals=0,
        ),
    )(idx, coefs, fields, fields, fields, *halos, *seeds)


def gram_kernel(n, idx_ref, *refs):
    ins, (own_ref, other_ref, fibre), folded = refs[:n], refs[n : n + 3], refs[n + 3]
    me, core = idx_ref[0], idx_ref[1]
    members, ppd, rows, yb = ins[0].shape
    half = n * rows // 2
    groups = half // (8 * n)
    for k in range(n):
        start = pl.multiple_of((me ^ k) * rows, rows)
        for m in range(members):
            for j in range(ppd):
                fibre[m, pl.ds(start, rows), j * yb : j * yb + yb] = ins[k][m, j]
    r = lax.broadcasted_iota(jnp.int32, (half, half), 0)
    c = lax.broadcasted_iota(jnp.int32, (half, half), 1)
    contract = (((1,), (1,)), ((), ()))
    for m in range(members):
        upper = fibre[m, :half, :]
        lower = fibre[m, half:, :]
        dot = functools.partial(
            lax.dot_general, dimension_numbers=contract, precision=highest, preferred_element_type=f32
        )
        cross = dot(upper, lower)
        first = dot(upper, upper)
        second = dot(lower, lower)
        packed = jnp.where(r <= c, first, second)
        diagonal = jnp.sum(jnp.where(r == c, second, 0.0), axis=0, keepdims=True)
        for d in range(n):
            for g in range(groups):
                at = (d * groups + g) * 8
                lo = g * 2 * half
                folded[m, d, :, lo : lo + half] = cross[at : at + 8, :]
                folded[m, d, :, lo + half : lo + 2 * half] = packed[at : at + 8, :]
            tile = (d * (half // 128)) // n
            folded[m, d, :, groups * 2 * half :] = jnp.broadcast_to(
                diagonal[:, tile * 128 : tile * 128 + 128], (8, 128)
            )
    own_ref[...] = folded[core]
    other_ref[...] = folded[1 - core]


def gram(idx, pieces):
    n = len(pieces)
    members, ppd, rows, yb = pieces[0].shape
    half = n * rows // 2
    wide = half // (8 * n) * 2 * half + 128
    chunk = jax.ShapeDtypeStruct((n, 8, wide), f32)
    fibre = jax.ShapeDtypeStruct((members, n * rows, ppd * yb), f32)
    return pl.pallas_call(
        functools.partial(gram_kernel, n),
        in_specs=[smem()] + [vmem()] * n,
        out_specs=[vmem()] * 3,
        out_shape=[chunk, chunk, fibre],
        scratch_shapes=[pltpu.VMEM((members, n, 8, wide), f32)],
        compiler_params=params_of(40),
    )(idx, *pieces)


def spread_kernel(n, idx_ref, own_ref, got_ref, *outs):
    for k in range(n):
        at = idx_ref[0] ^ k
        outs[k][...] = own_ref[at] + got_ref[at]


def spread(idx, own, got):
    n = own.shape[0]
    return pl.pallas_call(
        functools.partial(spread_kernel, n),
        in_specs=[smem(), vmem(), vmem()],
        out_specs=[vmem()] * n,
        out_shape=[jax.ShapeDtypeStruct(own.shape[1:], f32)] * n,
        compiler_params=params_of(16),
    )(idx, own, got)


def total_kernel(*refs):
    value = refs[0][...]
    for ref in refs[1:-1]:
        value = value + ref[...]
    refs[-1][...] = value


def total(pieces):
    return pl.pallas_call(
        total_kernel,
        in_specs=[vmem()] * len(pieces),
        out_specs=vmem(),
        out_shape=jax.ShapeDtypeStruct(pieces[0].shape, f32),
        compiler_params=params_of(16),
    )(*pieces)


def inverse_factor(cov):
    size = cov.shape[0]
    r = lax.broadcasted_iota(jnp.int32, (size, size), 0)
    c = lax.broadcasted_iota(jnp.int32, (size, size), 1)
    both = jnp.concatenate([cov, (r == c).astype(f32)], axis=1)
    groups = [both[g : g + 8, :] for g in range(0, size, 8)]
    sub = lax.broadcasted_iota(jnp.int32, (8, 2 * size), 0)
    for j in range(size):
        g, i = divmod(j, 8)
        pivot_row = groups[g][i : i + 1, :]
        scale = lax.rsqrt(pivot_row[:, j : j + 1])
        scaled = pivot_row * scale
        for h in range(g, size // 8):
            column = groups[h][:, j : j + 1] * scale
            update = groups[h] - column * scaled
            if h == g:
                update = jnp.where(sub > i, update, jnp.where(sub == i, scaled, groups[h]))
            groups[h] = update
    return jnp.concatenate([v[:, size:] for v in groups], axis=0)


def iterate_kernel(n, idx_ref, start_ref, *refs):
    ins, out_ref, folded, tails = refs[:n], refs[n], refs[n + 1], refs[n + 2]
    me, core = idx_ref[0], idx_ref[1]
    half = folded.shape[0]
    groups = half // (8 * n)
    for k in range(n):
        at = me ^ k
        for g in range(groups):
            place = pl.multiple_of(at * (8 * groups), 8) + 8 * g
            folded[pl.ds(place, 8), :] = ins[k][:, g * 2 * half : (g + 1) * 2 * half]
        tails[at] = ins[k][:, groups * 2 * half :]
    tiles = half // 128
    diagonal = jnp.concatenate([tails[t * n // tiles][0:1, :] for t in range(tiles)], axis=1)
    r = lax.broadcasted_iota(jnp.int32, (half, half), 0)
    c = lax.broadcasted_iota(jnp.int32, (half, half), 1)
    cross = folded[:, :half]
    packed = folded[:, half:]
    turned = packed.T
    first = jnp.where(r <= c, packed, turned)
    second = jnp.where(r > c, packed, jnp.where(r < c, turned, diagonal))
    dot = functools.partial(jnp.dot, precision=highest, preferred_element_type=f32)
    across = functools.partial(
        lax.dot_general,
        dimension_numbers=(((1,), (1,)), ((), ())),
        precision=highest,
        preferred_element_type=f32,
    )
    basis = start_ref[core]
    for _ in range(ITERS):
        a, b = basis[:, :half], basis[:, half:]
        image = jnp.concatenate([dot(a, first) + across(b, cross), dot(a, cross) + dot(b, second)], axis=1)
        basis = dot(inverse_factor(across(image, image)), image)
    out_ref[...] = basis


def iterate(idx, start, pieces):
    n = len(pieces)
    _, rank, size = start.shape
    half = size // 2
    return pl.pallas_call(
        functools.partial(iterate_kernel, n),
        in_specs=[smem()] + [vmem()] * (n + 1),
        out_specs=vmem(),
        out_shape=jax.ShapeDtypeStruct((rank, size), f32),
        scratch_shapes=[pltpu.VMEM((half, 2 * half), f32), pltpu.VMEM((n, 8, 128), f32)],
        compiler_params=params_of(40),
    )(idx, start, *pieces)


def project_kernel(n, idx_ref, own_ref, got_ref, fibre, basis_ref, *refs):
    outs, rows = refs[:n], refs[n]
    me, core = idx_ref[0], idx_ref[1]
    members = fibre.shape[0]
    share = outs[0].shape[1]
    basis_ref[core] = own_ref[...]
    basis_ref[1 - core] = got_ref[...]
    for m in range(members):
        value = jnp.dot(basis_ref[m], fibre[m], precision=highest, preferred_element_type=f32)
        for d in range(n):
            rows[d, m] = value[d * share : (d + 1) * share, :]
    for k in range(n):
        outs[k][...] = rows[me ^ k]


def project(idx, own, got, fibre, n):
    members, _, depth = fibre.shape
    rank, size = own.shape
    piece = (members, rank // n, depth)
    return pl.pallas_call(
        functools.partial(project_kernel, n),
        in_specs=[smem()] + [vmem()] * 3,
        out_specs=[vmem()] * (n + 1),
        out_shape=[jax.ShapeDtypeStruct((members, rank, size), f32)] + [jax.ShapeDtypeStruct(piece, f32)] * n,
        scratch_shapes=[pltpu.VMEM((n,) + piece, f32)],
        compiler_params=params_of(32),
    )(idx, own, got, fibre)


def gather_kernel(n, ppd, yb, idx_ref, *refs):
    ins, out, held = refs[:n], refs[n], refs[n + 1]
    members, share, nf, planes, cols = out.shape
    ysp = cols // yb
    for k in range(n):
        held[idx_ref[0] ^ k] = ins[k][...]
    for m in range(members):
        for s in range(share):
            for p in range(nf * planes):
                f, z = divmod(p, planes)
                for h in range(ysp):
                    piece = p * ysp + h
                    d, j = divmod(piece, ppd)
                    out[m, s, f, z : z + 1, h * yb : (h + 1) * yb] = held[
                        d, m, s : s + 1, j * yb : (j + 1) * yb
                    ]


def gather(idx, pieces, shape, ppd, yb):
    n = len(pieces)
    return pl.pallas_call(
        functools.partial(gather_kernel, n, ppd, yb),
        in_specs=[smem()] + [vmem()] * n,
        out_specs=vmem(),
        out_shape=jax.ShapeDtypeStruct(shape, f32),
        scratch_shapes=[pltpu.VMEM((n,) + pieces[0].shape, f32)],
        compiler_params=params_of(16),
    )(idx, *pieces)


def member_params(member_index, member_table):
    table_rows = member_table.shape[0]
    onehot = (member_index[:, None] == jnp.arange(table_rows, dtype=jnp.int32)[None, :]).astype(f32)
    return jnp.einsum("mp,pfk->mfk", onehot, member_table, precision=highest)


def exchange(pieces):
    n = lax.axis_size("gx")
    return [pieces[0]] + [
        lax.ppermute(pieces[k], "gx", [(i, i ^ k) for i in range(n)]) for k in range(1, n)
    ]


def swap_cores(value):
    return lax.ppermute(value, "gy", [(0, 1), (1, 0)])


def halos_of(idx, fields, planes, fb):
    n = lax.axis_size("gx")
    up = [(i, i + 1) for i in range(n - 1)]
    down = [(j, i) for i, j in up]
    top, bottom, side = edges(idx, fields, planes, fb)
    return (lax.ppermute(bottom, "gx", up), lax.ppermute(top, "gx", down), swap_cores(side))


def per_device(fields, member_index, member_table, seed_x, seed_y, seed_z, start_basis):
    n = lax.axis_size("gx")
    members, nf = fields.shape[:2]
    assert lax.axis_size("gy") == 2 and members == 2
    idx = jnp.stack([lax.axis_index("gx"), lax.axis_index("gy")]).astype(jnp.int32)
    params = member_params(member_index, member_table)
    kappa, mobility, gamma, strength = (params[:, :, k] for k in range(4))
    pace = time_step * mobility
    near = pace * kappa
    coefs = jnp.stack(
        [near, 1.0 - 6.0 * near + pace, pace * (1.0 - gamma), pace * gamma, source_gain * strength], axis=-1
    )
    seeds = (
        jnp.tile(seed_x.astype(f32), (1, 6))[:, None, :],
        jnp.tile(seed_y.astype(f32), (1, 6))[:, :, None],
        jnp.tile(seed_z.astype(f32), (1, 6))[:, None, :],
    )
    slab_halos = halos_of(idx, fields, ZS, nf)
    halos = halos_of(idx, fields, fields.shape[2], 1)
    slab = slab_step(idx, coefs, fields, slab_halos, seeds, n)
    pieces = exchange(slab)
    fields_next = bulk(idx, coefs, fields, halos, seeds)
    own, other, fibre = gram(idx, pieces)
    parts = exchange(spread(idx, own, swap_cores(other)))
    mine = total(parts)
    grams = exchange([mine] * n)
    start = jnp.swapaxes(start_basis, 1, 2)
    basis = iterate(idx, start, grams)
    bases, *rows = project(idx, basis, swap_cores(basis), fibre, n)
    ppd, yb, _ = slab_pieces(n, fields)
    share = start_basis.shape[2] // n
    core = gather(idx, exchange(rows), (members, share, nf, ZS, fields.shape[4]), ppd, yb)
    return (fields_next, jnp.swapaxes(bases, 1, 2), core)


def solution(mesh):
    placed = (
        P("grp", None, None, "gx", "gy"),
        P("grp"),
        P(),
        P("grp", None),
        P("grp", None),
        P("grp", None),
        P("grp", None, None),
    )
    return jax.shard_map(
        per_device,
        mesh=mesh,
        in_specs=placed,
        out_specs=(
            P("grp", None, None, "gx", "gy"),
            P("grp", None, None),
            P("grp", "gx", None, None, "gy"),
        ),
        check_vma=False,
    )
```

```python
import functools
import jax
import jax.numpy as jnp
from jax import lax
from jax.experimental import pallas as pl
from jax.experimental.pallas import tpu as pltpu
from jax.sharding import PartitionSpec as P

ZS = 4
ITERS = 3
ZB = 8

highest = lax.Precision.HIGHEST
time_step = 0.05
bump_width = 18.0
source_gain = 0.5
f32 = jnp.float32
bf16 = jnp.bfloat16
MIB = 1 << 20


def smem():
    return pl.BlockSpec(memory_space=pltpu.SMEM)


def vmem():
    return pl.BlockSpec(memory_space=pltpu.VMEM)


def params_of(limit):
    return pltpu.CompilerParams(vmem_limit_bytes=limit * MIB)


def split3(value):
    high = value.astype(bf16)
    rest = value - high.astype(f32)
    middle = rest.astype(bf16)
    low = (rest - middle.astype(f32)).astype(bf16)
    return high, middle, low


def edges_kernel(idx_ref, half_ref, side_ref):
    fb, planes, rows = half_ref.shape[1:4]
    lane = lax.broadcasted_iota(jnp.int32, (rows, 128), 1)
    offset = jnp.where(idx_ref[1] == 0, 1, 0)
    for f in range(fb):
        side = jnp.zeros((rows, 128), f32)
        for z in range(planes):
            turned = pltpu.roll(half_ref[0, f, z], z + offset, 1)
            side = jnp.where(lane == z, turned, side)
        side_ref[0, f] = side


def edges(idx, fields, planes, fb):
    m, f, _, rows, cols = fields.shape
    tail = cols // 128 - 1
    return pl.pallas_call(
        edges_kernel,
        grid_spec=pltpu.PrefetchScalarGridSpec(
            num_scalar_prefetch=1,
            grid=(m, f // fb),
            in_specs=[
                pl.BlockSpec(
                    (1, fb, planes, rows, 128),
                    lambda i, j, s: (i, j, 0, 0, jnp.where(s[1] == 0, tail, 0)),
                ),
            ],
            out_specs=pl.BlockSpec((1, fb, rows, 128), lambda i, j, s: (i, j, 0, 0)),
        ),
        out_shape=jax.ShapeDtypeStruct((m, f, rows, 128), f32),
        compiler_params=params_of(32),
        cost_estimate=pl.CostEstimate(
            flops=m * f * planes * rows * 256,
            bytes_accessed=m * f * planes * rows * 128 * 4,
            transcendentals=0,
        ),
    )(idx, fields)


def step_block(idx_ref, coef_ref, refs, zb, z0, m, store):
    now, before, after, yh, sx, sy, sz = refs
    nf, rows, cols = now.shape[1], now.shape[3], now.shape[4]
    tiles = cols // 128
    wide = sx.shape[-1]
    seeds = wide // 6
    x_start = idx_ref[0] * rows
    y_start = idx_ref[1] * cols
    along_x = (x_start + lax.broadcasted_iota(jnp.int32, (rows, wide), 0)).astype(f32)
    bump_x = jnp.exp(-jnp.square(along_x - sx[0]) / bump_width)
    along_y = (y_start + lax.broadcasted_iota(jnp.int32, (wide, cols), 1)).astype(f32)
    high, middle, low = split3(jnp.exp(-jnp.square(along_y - sy[0]) / bump_width))
    part = lax.broadcasted_iota(jnp.int32, (wide, cols), 0) // seeds
    right = jnp.where(
        part == 3,
        low.astype(f32),
        jnp.where((part == 1) | (part == 5), middle.astype(f32), high.astype(f32)),
    ).astype(bf16)
    group = lax.broadcasted_iota(jnp.int32, (rows, wide), 1) // seeds
    use_low = group == 4
    use_middle = (group == 2) | (group == 5)
    lane = lax.broadcasted_iota(jnp.int32, (8, 128), 1)
    row = lax.broadcasted_iota(jnp.int32, (8, cols), 0)
    is_left = lane == 0
    is_right = lane == 127
    is_top = row == 0
    is_bottom = row == 7
    at_end = idx_ref[1] == 0
    gain_left = jnp.where(at_end, 0.0, 1.0).astype(f32)
    gain_right = jnp.where(at_end, 1.0, 0.0).astype(f32)
    coefs = [[coef_ref[m, f, k] for k in range(5)] for f in range(nf)]

    def plane(z, below_of, above_of):
        along_z = (z0 + z).astype(f32) if not isinstance(z0 + z, int) else f32(z0 + z)
        bump_z = jnp.exp(-jnp.square(along_z - sz[0]) / bump_width)
        high, middle, low = split3(bump_x * bump_z)
        left = jnp.where(
            use_low, low.astype(f32), jnp.where(use_middle, middle.astype(f32), high.astype(f32))
        ).astype(bf16)
        source = jnp.dot(left, right, preferred_element_type=f32)
        shift = jnp.where(at_end, 127 - (z0 + z), 128 - (z0 + z))
        shift = jnp.where(shift == 128, 0, shift)
        for r in range(0, rows, 8):
            cells = [now[0, f, z, r : r + 8, :] for f in range(nf)]
            squared = [c * c for c in cells]
            squares = squared[0]
            for f in range(1, nf):
                squares = squares + squared[f]
            src = source[r : r + 8, :]
            for f in range(nf):
                c = cells[f]
                a, c0, c1, c2, s = coefs[f]
                if r == 0:
                    over = jnp.zeros((1, cols), f32)
                else:
                    over = now[0, f, z, r - 1 : r, :]
                if r + 8 == rows:
                    under = jnp.zeros((1, cols), f32)
                else:
                    under = now[0, f, z, r + 8 : r + 9, :]
                up = jnp.where(is_top, over, pltpu.roll(c, 1, 0))
                down = jnp.where(is_bottom, under, pltpu.roll(c, 7, 0))
                halo = pltpu.roll(yh[0, f, r : r + 8, :], shift, 1)
                parts = [c[:, 128 * t : 128 * t + 128] for t in range(tiles)]
                fwd = [pltpu.roll(p, 1, 1) for p in parts]
                bwd = [pltpu.roll(p, 127, 1) for p in parts]
                side = []
                for t in range(tiles):
                    from_left = halo * gain_left if t == 0 else fwd[t - 1]
                    from_right = halo * gain_right if t == tiles - 1 else bwd[t + 1]
                    side.append(
                        jnp.where(is_left, from_left, fwd[t])
                        + jnp.where(is_right, from_right, bwd[t])
                    )
                near = (
                    jnp.concatenate(side, axis=1)
                    + (up + down)
                    + (below_of(f, r) + above_of(f, r))
                )
                value = a * near + c * (c0 - c1 * squared[f] - c2 * squares) + s * src
                store(f, z, r, value)

    def prior(z):
        return lambda f, r: now[0, f, z - 1, r : r + 8, :]

    def later(z):
        return lambda f, r: now[0, f, z + 1, r : r + 8, :]

    plane(0, lambda f, r: before[0, f, 0, r : r + 8, :], later(0))

    def body(z, carry):
        plane(z, prior(z), later(z))
        return carry

    lax.fori_loop(1, zb - 1, body, 0)
    plane(zb - 1, prior(zb - 1), lambda f, r: after[0, f, 0, r : r + 8, :])


def bulk_kernel(idx_ref, coef_ref, *refs):
    now = refs[0]
    out, top, bottom = refs[-3:]
    nf, rows = now.shape[1], now.shape[3]
    m, t = pl.program_id(0), pl.program_id(1)
    for f in range(nf):
        for z in range(ZB):
            top[0, f, z : z + 1, :] = now[0, f, z, 0:1, :]
            bottom[0, f, z : z + 1, :] = now[0, f, z, rows - 1 : rows, :]

    def store(f, z, r, value):
        out[0, f, z, r : r + 8, :] = value

    step_block(idx_ref, coef_ref, refs[:-3], ZB, t * ZB, m, store)


def step_specs(fields, zb, wide, place):
    m, f, nz, rows, cols = fields.shape

    def at(shape, index):
        return pl.BlockSpec(shape, lambda *g: index(*place(*g), None))

    return [
        at((1, f, zb, rows, cols), lambda i, t, s: (i, 0, t, 0, 0)),
        at((1, f, 1, rows, cols), lambda i, t, s: (i, 0, jnp.maximum(t * zb - 1, 0), 0, 0)),
        at((1, f, 1, rows, cols), lambda i, t, s: (i, 0, jnp.minimum(t * zb + zb, nz - 1), 0, 0)),
        at((1, f, rows, 128), lambda i, t, s: (i, 0, 0, 0)),
        at((1, 1, wide), lambda i, t, s: (i, 0, 0)),
        at((1, wide, 1), lambda i, t, s: (i, 0, 0)),
        at((1, 1, wide), lambda i, t, s: (i, 0, 0)),
    ]


def bulk(idx, coefs, fields, side, seeds):
    m, f, nz, rows, cols = fields.shape
    wide = seeds[0].shape[-1]
    specs = step_specs(fields, ZB, wide, lambda i, t, s: (i, t))
    return pl.pallas_call(
        bulk_kernel,
        grid_spec=pltpu.PrefetchScalarGridSpec(
            num_scalar_prefetch=1,
            grid=(m, nz // ZB),
            in_specs=[smem()] + specs,
            out_specs=[
                pl.BlockSpec((1, f, ZB, rows, cols), lambda i, t, s: (i, 0, t, 0, 0)),
                pl.BlockSpec((1, f, ZB, cols), lambda i, t, s: (i, 0, t, 0)),
                pl.BlockSpec((1, f, ZB, cols), lambda i, t, s: (i, 0, t, 0)),
            ],
        ),
        out_shape=[
            jax.ShapeDtypeStruct(fields.shape, f32),
            jax.ShapeDtypeStruct((m, f, nz, cols), f32),
            jax.ShapeDtypeStruct((m, f, nz, cols), f32),
        ],
        compiler_params=params_of(40),
        cost_estimate=pl.CostEstimate(
            flops=fields.size * 30, bytes_accessed=fields.size * 10, transcendentals=0
        ),
    )(idx, coefs, fields, fields, fields, side, *seeds)


def slab_kernel(n, ppd, yb, idx_ref, coef_ref, *refs):
    ins, out = refs[:7], refs[7]
    now = ins[0]
    nf, rows = now.shape[1], now.shape[3]
    m = pl.program_id(0)
    ysp = now.shape[4] // yb
    members = (out.shape[1] - 8) // (ppd * rows)

    def store(f, z, r, value):
        for h in range(ysp):
            d, j = divmod((f * ZS + z) * ysp + h, ppd)
            at = pl.multiple_of((m * ppd + j) * rows, rows) + r
            out[d, pl.ds(at, 8), :] = value[:, h * yb : h * yb + yb]

    step_block(idx_ref, coef_ref, ins, ZS, 0, m, store)
    for i in range(members):

        @pl.when(m == i)
        def _():
            for f in range(nf):
                for z in range(ZS):
                    for h in range(ysp):
                        d, j = divmod((f * ZS + z) * ysp + h, ppd)
                        at = members * ppd * rows + 2 * (i * ppd + j)
                        out[d, at : at + 1, :] = now[0, f, z, 0:1, h * yb : h * yb + yb]
                        out[d, at + 1 : at + 2, :] = now[0, f, z, rows - 1 : rows, h * yb : h * yb + yb]


def slab_pieces(n, fields):
    _, f, _, _, cols = fields.shape
    count = f * ZS
    ysp = max(1, n // count)
    return max(1, count // n), cols // ysp, count * ysp


def slab_step(idx, coefs, fields, side, seeds, n):
    m, f, nz, rows, cols = fields.shape
    wide = seeds[0].shape[-1]
    ppd, yb, pieces = slab_pieces(n, fields)
    piece = jax.ShapeDtypeStruct((n, m * ppd * rows + 8, yb), f32)
    specs = step_specs(fields, ZS, wide, lambda i, t, s: (i, t))
    return pl.pallas_call(
        functools.partial(slab_kernel, n, ppd, yb),
        grid_spec=pltpu.PrefetchScalarGridSpec(
            num_scalar_prefetch=1,
            grid=(m, 1),
            in_specs=[smem()] + specs,
            out_specs=pl.BlockSpec(piece.shape, lambda i, t, s: (0, 0, 0)),
        ),
        out_shape=piece,
        compiler_params=params_of(32),
        cost_estimate=pl.CostEstimate(
            flops=m * f * ZS * rows * cols * 30,
            bytes_accessed=m * f * ZS * rows * cols * 10,
            transcendentals=0,
        ),
    )(idx, coefs, fields, fields, fields, side, *seeds)


def mend_kernel(coef_ref, value_ref, before_ref, after_ref, out_ref):
    m, f, end = pl.program_id(0), pl.program_id(1), pl.program_id(2)
    a = coef_ref[m, f, 0]
    planes = out_ref.shape[2]
    out_ref[...] = value_ref[...]

    @pl.when(end == 0)
    def _():
        for z in range(planes):
            out_ref[0, 0, z, 0:1, :] = value_ref[0, 0, z, 0:1, :] + a * before_ref[0, 0, z : z + 1, :]

    @pl.when(end == 1)
    def _():
        for z in range(planes):
            out_ref[0, 0, z, 7:8, :] = value_ref[0, 0, z, 7:8, :] + a * after_ref[0, 0, z : z + 1, :]


def mend(coefs, value, before, after):
    m, f, nz, rows, cols = value.shape
    last = rows // 8 - 1
    block = pl.BlockSpec((1, 1, nz, 8, cols), lambda i, j, e: (i, j, 0, e * last, 0))
    halo = pl.BlockSpec((1, 1, nz, cols), lambda i, j, e: (i, j, 0, 0))
    return pl.pallas_call(
        mend_kernel,
        grid=(m, f, 2),
        in_specs=[smem(), block, halo, halo],
        out_specs=block,
        out_shape=jax.ShapeDtypeStruct(value.shape, f32),
        input_output_aliases={1: 0},
        compiler_params=params_of(16),
        cost_estimate=pl.CostEstimate(
            flops=m * f * nz * 4 * cols, bytes_accessed=m * f * nz * 32 * cols * 4, transcendentals=0
        ),
    )(coefs, value, before, after)


def gram_kernel(n, ppd, ysp, idx_ref, coef_ref, *refs):
    ins, own_ref, other_ref, fibre, folded = refs
    me, core = idx_ref[0], idx_ref[1]
    yb = ins.shape[2]
    members = fibre.shape[0]
    rows = fibre.shape[1] // n
    half = n * rows // 2
    groups = half // (8 * n)
    edge = members * ppd * rows
    for b in range(n):
        for m in range(members):
            for j in range(ppd):
                at = (m * ppd + j) * rows
                fibre[m, b * rows : (b + 1) * rows, j * yb : j * yb + yb] = ins[b, at : at + rows, :]
    for m in range(members):
        for j in range(ppd):
            a = coef_ref[m, (me * ppd + j) // (ysp * ZS), 0]
            at = edge + 2 * (m * ppd + j)
            here = slice(j * yb, j * yb + yb)
            for b in range(n - 1):
                low, up = (b + 1) * rows - 1, (b + 1) * rows
                fibre[m, low : low + 1, here] += a * ins[b + 1, at : at + 1, :]
                fibre[m, up : up + 1, here] += a * ins[b, at + 1 : at + 2, :]
    r = lax.broadcasted_iota(jnp.int32, (half, half), 0)
    c = lax.broadcasted_iota(jnp.int32, (half, half), 1)
    contract = (((1,), (1,)), ((), ()))
    for m in range(members):
        upper = fibre[m, :half, :]
        lower = fibre[m, half:, :]
        dot = functools.partial(
            lax.dot_general, dimension_numbers=contract, precision=highest, preferred_element_type=f32
        )
        cross = dot(upper, lower)
        first = dot(upper, upper)
        second = dot(lower, lower)
        packed = jnp.where(r <= c, first, second)
        diagonal = jnp.sum(jnp.where(r == c, second, 0.0), axis=0, keepdims=True)
        for d in range(n):
            for g in range(groups):
                at = (d * groups + g) * 8
                lo = g * 2 * half
                folded[m, d, :, lo : lo + half] = cross[at : at + 8, :]
                folded[m, d, :, lo + half : lo + 2 * half] = packed[at : at + 8, :]
            tile = (d * (half // 128)) // n
            folded[m, d, :, groups * 2 * half :] = jnp.broadcast_to(
                diagonal[:, tile * 128 : tile * 128 + 128], (8, 128)
            )
    own_ref[...] = folded[core]
    other_ref[...] = folded[1 - core]


def gram(idx, coefs, pieces, members, ppd, ysp):
    n, length, yb = pieces.shape
    rows = (length - 8) // (members * ppd)
    half = n * rows // 2
    wide = half // (8 * n) * 2 * half + 128
    chunk = jax.ShapeDtypeStruct((n, 8, wide), f32)
    fibre = jax.ShapeDtypeStruct((members, n * rows, ppd * yb), f32)
    return pl.pallas_call(
        functools.partial(gram_kernel, n, ppd, ysp),
        in_specs=[smem(), smem(), vmem()],
        out_specs=[vmem()] * 3,
        out_shape=[chunk, chunk, fibre],
        scratch_shapes=[pltpu.VMEM((members, n, 8, wide), f32)],
        compiler_params=params_of(40),
    )(idx, coefs, pieces)


def spread_kernel(n, idx_ref, own_ref, got_ref, *outs):
    for k in range(n):
        at = idx_ref[0] ^ k
        outs[k][...] = own_ref[at] + got_ref[at]


def spread(idx, own, got):
    n = own.shape[0]
    return pl.pallas_call(
        functools.partial(spread_kernel, n),
        in_specs=[smem(), vmem(), vmem()],
        out_specs=[vmem()] * n,
        out_shape=[jax.ShapeDtypeStruct(own.shape[1:], f32)] * n,
        compiler_params=params_of(16),
    )(idx, own, got)


def total_kernel(*refs):
    value = refs[0][...]
    for ref in refs[1:-1]:
        value = value + ref[...]
    refs[-1][...] = value


def total(pieces):
    return pl.pallas_call(
        total_kernel,
        in_specs=[vmem()] * len(pieces),
        out_specs=vmem(),
        out_shape=jax.ShapeDtypeStruct(pieces[0].shape, f32),
        compiler_params=params_of(16),
    )(*pieces)


def inverse_factor(cov):
    size = cov.shape[0]
    r = lax.broadcasted_iota(jnp.int32, (size, size), 0)
    c = lax.broadcasted_iota(jnp.int32, (size, size), 1)
    both = jnp.concatenate([cov, (r == c).astype(f32)], axis=1)
    groups = [both[g : g + 8, :] for g in range(0, size, 8)]
    sub = lax.broadcasted_iota(jnp.int32, (8, 2 * size), 0)
    for j in range(size):
        g, i = divmod(j, 8)
        pivot_row = groups[g][i : i + 1, :]
        scale = lax.rsqrt(pivot_row[:, j : j + 1])
        scaled = pivot_row * scale
        for h in range(g, size // 8):
            column = groups[h][:, j : j + 1] * scale
            update = groups[h] - column * scaled
            if h == g:
                update = jnp.where(sub > i, update, jnp.where(sub == i, scaled, groups[h]))
            groups[h] = update
    return jnp.concatenate([v[:, size:] for v in groups], axis=0)


def iterate_kernel(n, idx_ref, start_ref, *refs):
    ins, out_ref, folded, tails = refs[:n], refs[n], refs[n + 1], refs[n + 2]
    me, core = idx_ref[0], idx_ref[1]
    half = folded.shape[0]
    groups = half // (8 * n)
    for k in range(n):
        at = me ^ k
        for g in range(groups):
            place = pl.multiple_of(at * (8 * groups), 8) + 8 * g
            folded[pl.ds(place, 8), :] = ins[k][:, g * 2 * half : (g + 1) * 2 * half]
        tails[at] = ins[k][:, groups * 2 * half :]
    tiles = half // 128
    diagonal = jnp.concatenate([tails[t * n // tiles][0:1, :] for t in range(tiles)], axis=1)
    r = lax.broadcasted_iota(jnp.int32, (half, half), 0)
    c = lax.broadcasted_iota(jnp.int32, (half, half), 1)
    cross = folded[:, :half]
    packed = folded[:, half:]
    turned = packed.T
    first = jnp.where(r <= c, packed, turned)
    second = jnp.where(r > c, packed, jnp.where(r < c, turned, diagonal))
    dot = functools.partial(jnp.dot, precision=highest, preferred_element_type=f32)
    across = functools.partial(
        lax.dot_general,
        dimension_numbers=(((1,), (1,)), ((), ())),
        precision=highest,
        preferred_element_type=f32,
    )
    basis = start_ref[core]
    for _ in range(ITERS):
        a, b = basis[:, :half], basis[:, half:]
        image = jnp.concatenate([dot(a, first) + across(b, cross), dot(a, cross) + dot(b, second)], axis=1)
        basis = dot(inverse_factor(across(image, image)), image)
    out_ref[...] = basis


def iterate(idx, start, pieces):
    n = len(pieces)
    _, rank, size = start.shape
    half = size // 2
    return pl.pallas_call(
        functools.partial(iterate_kernel, n),
        in_specs=[smem()] + [vmem()] * (n + 1),
        out_specs=vmem(),
        out_shape=jax.ShapeDtypeStruct((rank, size), f32),
        scratch_shapes=[pltpu.VMEM((half, 2 * half), f32), pltpu.VMEM((n, 8, 128), f32)],
        compiler_params=params_of(40),
    )(idx, start, *pieces)


def project_kernel(n, idx_ref, own_ref, got_ref, fibre, basis_ref, out_ref):
    core = idx_ref[1]
    share = out_ref.shape[2]
    basis_ref[core] = own_ref[...]
    basis_ref[1 - core] = got_ref[...]
    for m in range(fibre.shape[0]):
        value = jnp.dot(basis_ref[m], fibre[m], precision=highest, preferred_element_type=f32)
        for d in range(n):
            out_ref[d, m] = value[d * share : (d + 1) * share, :]


def project(idx, own, got, fibre, n):
    members, _, depth = fibre.shape
    rank, size = own.shape
    return pl.pallas_call(
        functools.partial(project_kernel, n),
        in_specs=[smem()] + [vmem()] * 3,
        out_specs=[vmem()] * 2,
        out_shape=[
            jax.ShapeDtypeStruct((members, rank, size), f32),
            jax.ShapeDtypeStruct((n, members, rank // n, depth), f32),
        ],
        compiler_params=params_of(32),
    )(idx, own, got, fibre)


def gather_kernel(ppd, yb, held, out):
    members, share, nf, planes, cols = out.shape
    ysp = cols // yb
    for m in range(members):
        for s in range(share):
            for p in range(nf * planes):
                f, z = divmod(p, planes)
                for h in range(ysp):
                    d, j = divmod(p * ysp + h, ppd)
                    out[m, s, f, z : z + 1, h * yb : (h + 1) * yb] = held[
                        d, m, s : s + 1, j * yb : (j + 1) * yb
                    ]


def gather(pieces, shape, ppd, yb):
    return pl.pallas_call(
        functools.partial(gather_kernel, ppd, yb),
        in_specs=[vmem()],
        out_specs=vmem(),
        out_shape=jax.ShapeDtypeStruct(shape, f32),
        compiler_params=params_of(16),
    )(pieces)


def member_params(member_index, member_table):
    table_rows = member_table.shape[0]
    onehot = (member_index[:, None] == jnp.arange(table_rows, dtype=jnp.int32)[None, :]).astype(f32)
    return jnp.einsum("mp,pfk->mfk", onehot, member_table, precision=highest)


def exchange(pieces):
    n = lax.axis_size("gx")
    return [pieces[0]] + [
        lax.ppermute(pieces[k], "gx", [(i, i ^ k) for i in range(n)]) for k in range(1, n)
    ]


def swap_cores(value):
    return lax.ppermute(value, "gy", [(0, 1), (1, 0)])


def per_device(fields, member_index, member_table, seed_x, seed_y, seed_z, start_basis):
    n = lax.axis_size("gx")
    members, nf = fields.shape[:2]
    assert lax.axis_size("gy") == 2 and members == 2
    idx = jnp.stack([lax.axis_index("gx"), lax.axis_index("gy")]).astype(jnp.int32)
    params = member_params(member_index, member_table)
    kappa, mobility, gamma, strength = (params[:, :, k] for k in range(4))
    pace = time_step * mobility
    near = pace * kappa
    coefs = jnp.stack(
        [near, 1.0 - 6.0 * near + pace, pace * (1.0 - gamma), pace * gamma, source_gain * strength], axis=-1
    )
    seeds = (
        jnp.tile(seed_x.astype(f32), (1, 6))[:, None, :],
        jnp.tile(seed_y.astype(f32), (1, 6))[:, :, None],
        jnp.tile(seed_z.astype(f32), (1, 6))[:, None, :],
    )
    ppd, yb, _ = slab_pieces(n, fields)
    up = [(i, i + 1) for i in range(n - 1)]
    down = [(j, i) for i, j in up]
    slab_side = swap_cores(edges(idx, fields, ZS, nf))
    pieces = lax.all_to_all(slab_step(idx, coefs, fields, slab_side, seeds, n), "gx", 0, 0)
    side = swap_cores(edges(idx, fields, fields.shape[2], 2))
    value, top, bottom = bulk(idx, coefs, fields, side, seeds)
    pieces, value = lax.optimization_barrier((pieces, value))
    own, other, fibre = gram(idx, coefs, pieces, members, ppd, fields.shape[4] // yb)
    parts = exchange(spread(idx, own, swap_cores(other)))
    mine = total(parts)
    grams = exchange([mine] * n)
    grams, top, bottom = lax.optimization_barrier((grams, top, bottom))
    before, after = lax.ppermute(bottom, "gx", up), lax.ppermute(top, "gx", down)
    start = jnp.swapaxes(start_basis, 1, 2)
    basis = iterate(idx, start, grams)
    basis, before, after = lax.optimization_barrier((basis, before, after))
    bases, rows = project(idx, basis, swap_cores(basis), fibre, n)
    fields_next = mend(coefs, value, before, after)
    share = start_basis.shape[2] // n
    core = gather(lax.all_to_all(rows, "gx", 0, 0), (members, share, nf, ZS, fields.shape[4]), ppd, yb)
    return (fields_next, jnp.swapaxes(bases, 1, 2), core)


def solution(mesh):
    placed = (
        P("grp", None, None, "gx", "gy"),
        P("grp"),
        P(),
        P("grp", None),
        P("grp", None),
        P("grp", None),
        P("grp", None, None),
    )
    return jax.shard_map(
        per_device,
        mesh=mesh,
        in_specs=placed,
        out_specs=(
            P("grp", None, None, "gx", "gy"),
            P("grp", None, None),
            P("grp", "gx", None, None, "gy"),
        ),
        check_vma=False,
    )
```

```python
import functools
import jax
import jax.numpy as jnp
from jax import lax
from jax.experimental import pallas as pl
from jax.experimental.pallas import tpu as pltpu
from jax.sharding import PartitionSpec as P

ZS = 4
ITERS = 3
ZB = 8

highest = lax.Precision.HIGHEST
time_step = 0.05
bump_width = 18.0
source_gain = 0.5
f32 = jnp.float32
bf16 = jnp.bfloat16
MIB = 1 << 20


def smem():
    return pl.BlockSpec(memory_space=pltpu.SMEM)


def vmem():
    return pl.BlockSpec(memory_space=pltpu.VMEM)


def params_of(limit):
    return pltpu.CompilerParams(vmem_limit_bytes=limit * MIB)


def split3(value):
    high = value.astype(bf16)
    rest = value - high.astype(f32)
    middle = rest.astype(bf16)
    low = (rest - middle.astype(f32)).astype(bf16)
    return high, middle, low


def stacked(parts):
    return jnp.concatenate(parts, axis=0)


def apply3(left, right):
    rows = left[0].shape[0]
    first = jnp.dot(stacked(left), right[0], preferred_element_type=f32)
    second = jnp.dot(stacked(left[:2]), right[1], preferred_element_type=f32)
    third = jnp.dot(left[0], right[2], preferred_element_type=f32)
    small = first[2 * rows :] + second[rows:] + third
    return first[:rows] + (first[rows : 2 * rows] + second[:rows] + small)


def square3(parts):
    rows = parts[0].shape[0]
    whole = stacked(parts)
    every = lax.dot_general(whole, whole, (((1,), (1,)), ((), ())), preferred_element_type=f32)

    def piece(i, j):
        return every[i * rows : (i + 1) * rows, j * rows : (j + 1) * rows]

    return piece(0, 0) + (piece(0, 1) + piece(1, 0) + (piece(0, 2) + piece(2, 0) + piece(1, 1)))


def edges_kernel(idx_ref, half_ref, side_ref):
    mb, fb, planes, rows = half_ref.shape[:4]
    lane = lax.broadcasted_iota(jnp.int32, (rows, 128), 1)
    offset = jnp.where(idx_ref[1] == 0, 1, 0)
    for m in range(mb):
        for f in range(fb):
            side = jnp.zeros((rows, 128), f32)
            for z in range(planes):
                turned = pltpu.roll(half_ref[m, f, z], z + offset, 1)
                side = jnp.where(lane == z, turned, side)
            side_ref[m, f] = side


def edges(idx, fields, planes, mb, fb):
    m, f, _, rows, cols = fields.shape
    tail = cols // 128 - 1
    return pl.pallas_call(
        edges_kernel,
        grid_spec=pltpu.PrefetchScalarGridSpec(
            num_scalar_prefetch=1,
            grid=(m // mb, f // fb),
            in_specs=[
                pl.BlockSpec(
                    (mb, fb, planes, rows, 128),
                    lambda i, j, s: (i, j, 0, 0, jnp.where(s[1] == 0, tail, 0)),
                ),
            ],
            out_specs=pl.BlockSpec((mb, fb, rows, 128), lambda i, j, s: (i, j, 0, 0)),
        ),
        out_shape=jax.ShapeDtypeStruct((m, f, rows, 128), f32),
        compiler_params=params_of(32),
        cost_estimate=pl.CostEstimate(
            flops=m * f * planes * rows * 256,
            bytes_accessed=m * f * planes * rows * 128 * 4,
            transcendentals=0,
        ),
    )(idx, fields)


def step_block(idx_ref, coef_ref, refs, zb, z0, m, store):
    now, before, after, yh, sx, sy, sz = refs
    nf, rows, cols = now.shape[1], now.shape[3], now.shape[4]
    tiles = cols // 128
    wide = sx.shape[-1]
    seeds = wide // 6
    x_start = idx_ref[0] * rows
    y_start = idx_ref[1] * cols
    along_x = (x_start + lax.broadcasted_iota(jnp.int32, (rows, wide), 0)).astype(f32)
    bump_x = jnp.exp(-jnp.square(along_x - sx[0]) / bump_width)
    along_y = (y_start + lax.broadcasted_iota(jnp.int32, (wide, cols), 1)).astype(f32)
    high, middle, low = split3(jnp.exp(-jnp.square(along_y - sy[0]) / bump_width))
    part = lax.broadcasted_iota(jnp.int32, (wide, cols), 0) // seeds
    right = jnp.where(
        part == 3,
        low.astype(f32),
        jnp.where((part == 1) | (part == 5), middle.astype(f32), high.astype(f32)),
    ).astype(bf16)
    group = lax.broadcasted_iota(jnp.int32, (rows, wide), 1) // seeds
    use_low = group == 4
    use_middle = (group == 2) | (group == 5)
    lane = lax.broadcasted_iota(jnp.int32, (8, 128), 1)
    row = lax.broadcasted_iota(jnp.int32, (8, cols), 0)
    is_left = lane == 0
    is_right = lane == 127
    is_top = row == 0
    is_bottom = row == 7
    at_end = idx_ref[1] == 0
    gain_left = jnp.where(at_end, 0.0, 1.0).astype(f32)
    gain_right = jnp.where(at_end, 1.0, 0.0).astype(f32)
    coefs = [[coef_ref[m, f, k] for k in range(5)] for f in range(nf)]

    def plane(z, below_of, above_of):
        along_z = (z0 + z).astype(f32) if not isinstance(z0 + z, int) else f32(z0 + z)
        bump_z = jnp.exp(-jnp.square(along_z - sz[0]) / bump_width)
        high, middle, low = split3(bump_x * bump_z)
        left = jnp.where(
            use_low, low.astype(f32), jnp.where(use_middle, middle.astype(f32), high.astype(f32))
        ).astype(bf16)
        source = jnp.dot(left, right, preferred_element_type=f32)
        shift = jnp.where(at_end, 127 - (z0 + z), 128 - (z0 + z))
        shift = jnp.where(shift == 128, 0, shift)
        for r in range(0, rows, 8):
            cells = [now[0, f, z, r : r + 8, :] for f in range(nf)]
            squared = [c * c for c in cells]
            squares = squared[0]
            for f in range(1, nf):
                squares = squares + squared[f]
            src = source[r : r + 8, :]
            for f in range(nf):
                c = cells[f]
                a, c0, c1, c2, s = coefs[f]
                if r == 0:
                    over = jnp.zeros((1, cols), f32)
                else:
                    over = now[0, f, z, r - 1 : r, :]
                if r + 8 == rows:
                    under = jnp.zeros((1, cols), f32)
                else:
                    under = now[0, f, z, r + 8 : r + 9, :]
                up = jnp.where(is_top, over, pltpu.roll(c, 1, 0))
                down = jnp.where(is_bottom, under, pltpu.roll(c, 7, 0))
                halo = pltpu.roll(yh[0, f, r : r + 8, :], shift, 1)
                parts = [c[:, 128 * t : 128 * t + 128] for t in range(tiles)]
                fwd = [pltpu.roll(p, 1, 1) for p in parts]
                bwd = [pltpu.roll(p, 127, 1) for p in parts]
                side = []
                for t in range(tiles):
                    from_left = halo * gain_left if t == 0 else fwd[t - 1]
                    from_right = halo * gain_right if t == tiles - 1 else bwd[t + 1]
                    side.append(
                        jnp.where(is_left, from_left, fwd[t])
                        + jnp.where(is_right, from_right, bwd[t])
                    )
                near = (
                    jnp.concatenate(side, axis=1)
                    + (up + down)
                    + (below_of(f, r) + above_of(f, r))
                )
                value = a * near + c * (c0 - c1 * squared[f] - c2 * squares) + s * src
                store(f, z, r, value)

    def prior(z):
        return lambda f, r: now[0, f, z - 1, r : r + 8, :]

    def later(z):
        return lambda f, r: now[0, f, z + 1, r : r + 8, :]

    plane(0, lambda f, r: before[0, f, 0, r : r + 8, :], later(0))

    def body(z, carry):
        plane(z, prior(z), later(z))
        return carry

    lax.fori_loop(1, zb - 1, body, 0)
    plane(zb - 1, prior(zb - 1), lambda f, r: after[0, f, 0, r : r + 8, :])


def bulk_kernel(idx_ref, coef_ref, *refs):
    now = refs[0]
    out, top, bottom = refs[-3:]
    nf, rows = now.shape[1], now.shape[3]
    m, t = pl.program_id(0), pl.program_id(1)
    for f in range(nf):
        for z in range(ZB):
            top[0, f, z : z + 1, :] = now[0, f, z, 0:1, :]
            bottom[0, f, z : z + 1, :] = now[0, f, z, rows - 1 : rows, :]

    def store(f, z, r, value):
        out[0, f, z, r : r + 8, :] = value

    step_block(idx_ref, coef_ref, refs[:-3], ZB, t * ZB, m, store)


def step_specs(fields, zb, wide, place):
    m, f, nz, rows, cols = fields.shape

    def at(shape, index):
        return pl.BlockSpec(shape, lambda *g: index(*place(*g), None))

    return [
        at((1, f, zb, rows, cols), lambda i, t, s: (i, 0, t, 0, 0)),
        at((1, f, 1, rows, cols), lambda i, t, s: (i, 0, jnp.maximum(t * zb - 1, 0), 0, 0)),
        at((1, f, 1, rows, cols), lambda i, t, s: (i, 0, jnp.minimum(t * zb + zb, nz - 1), 0, 0)),
        at((1, f, rows, 128), lambda i, t, s: (i, 0, 0, 0)),
        at((1, 1, wide), lambda i, t, s: (i, 0, 0)),
        at((1, wide, 1), lambda i, t, s: (i, 0, 0)),
        at((1, 1, wide), lambda i, t, s: (i, 0, 0)),
    ]


def bulk(idx, coefs, fields, side, seeds):
    m, f, nz, rows, cols = fields.shape
    wide = seeds[0].shape[-1]
    specs = step_specs(fields, ZB, wide, lambda i, t, s: (i, t))
    return pl.pallas_call(
        bulk_kernel,
        grid_spec=pltpu.PrefetchScalarGridSpec(
            num_scalar_prefetch=1,
            grid=(m, nz // ZB),
            in_specs=[smem()] + specs,
            out_specs=[
                pl.BlockSpec((1, f, ZB, rows, cols), lambda i, t, s: (i, 0, t, 0, 0)),
                pl.BlockSpec((1, f, ZB, cols), lambda i, t, s: (i, 0, t, 0)),
                pl.BlockSpec((1, f, ZB, cols), lambda i, t, s: (i, 0, t, 0)),
            ],
        ),
        out_shape=[
            jax.ShapeDtypeStruct(fields.shape, f32),
            jax.ShapeDtypeStruct((m, f, nz, cols), f32),
            jax.ShapeDtypeStruct((m, f, nz, cols), f32),
        ],
        compiler_params=params_of(40),
        cost_estimate=pl.CostEstimate(
            flops=fields.size * 30, bytes_accessed=fields.size * 10, transcendentals=0
        ),
    )(idx, coefs, fields, fields, fields, side, *seeds)


def slab_kernel(n, ppd, yb, idx_ref, coef_ref, *refs):
    ins, out = refs[:7], refs[7]
    now = ins[0]
    nf, rows = now.shape[1], now.shape[3]
    m = pl.program_id(0)
    ysp = now.shape[4] // yb
    members = (out.shape[1] - 8) // (ppd * rows)

    def store(f, z, r, value):
        for h in range(ysp):
            d, j = divmod((f * ZS + z) * ysp + h, ppd)
            at = pl.multiple_of((m * ppd + j) * rows, rows) + r
            out[d, pl.ds(at, 8), :] = value[:, h * yb : h * yb + yb]

    step_block(idx_ref, coef_ref, ins, ZS, 0, m, store)
    for i in range(members):

        @pl.when(m == i)
        def _():
            for f in range(nf):
                for z in range(ZS):
                    for h in range(ysp):
                        d, j = divmod((f * ZS + z) * ysp + h, ppd)
                        at = members * ppd * rows + 2 * (i * ppd + j)
                        out[d, at : at + 1, :] = now[0, f, z, 0:1, h * yb : h * yb + yb]
                        out[d, at + 1 : at + 2, :] = now[0, f, z, rows - 1 : rows, h * yb : h * yb + yb]


def slab_pieces(n, fields):
    _, f, _, _, cols = fields.shape
    count = f * ZS
    ysp = max(1, n // count)
    return max(1, count // n), cols // ysp, count * ysp


def slab_step(idx, coefs, fields, side, seeds, n):
    m, f, nz, rows, cols = fields.shape
    wide = seeds[0].shape[-1]
    ppd, yb, pieces = slab_pieces(n, fields)
    piece = jax.ShapeDtypeStruct((n, m * ppd * rows + 8, yb), f32)
    specs = step_specs(fields, ZS, wide, lambda i, t, s: (i, t))
    return pl.pallas_call(
        functools.partial(slab_kernel, n, ppd, yb),
        grid_spec=pltpu.PrefetchScalarGridSpec(
            num_scalar_prefetch=1,
            grid=(m, 1),
            in_specs=[smem()] + specs,
            out_specs=pl.BlockSpec(piece.shape, lambda i, t, s: (0, 0, 0)),
        ),
        out_shape=piece,
        compiler_params=params_of(32),
        cost_estimate=pl.CostEstimate(
            flops=m * f * ZS * rows * cols * 30,
            bytes_accessed=m * f * ZS * rows * cols * 10,
            transcendentals=0,
        ),
    )(idx, coefs, fields, fields, fields, side, *seeds)


def mend_kernel(coef_ref, value_ref, before_ref, after_ref, out_ref):
    m, end = pl.program_id(0), pl.program_id(1)
    nf, planes = out_ref.shape[1:3]
    out_ref[...] = value_ref[...]

    @pl.when(end == 0)
    def _():
        for f in range(nf):
            a = coef_ref[m, f, 0]
            for z in range(planes):
                out_ref[0, f, z, 0:1, :] = value_ref[0, f, z, 0:1, :] + a * before_ref[0, f, z : z + 1, :]

    @pl.when(end == 1)
    def _():
        for f in range(nf):
            a = coef_ref[m, f, 0]
            for z in range(planes):
                out_ref[0, f, z, 7:8, :] = value_ref[0, f, z, 7:8, :] + a * after_ref[0, f, z : z + 1, :]


def mend(coefs, value, before, after):
    m, f, nz, rows, cols = value.shape
    last = rows // 8 - 1
    block = pl.BlockSpec((1, f, nz, 8, cols), lambda i, e: (i, 0, 0, e * last, 0))
    halo = pl.BlockSpec((1, f, nz, cols), lambda i, e: (i, 0, 0, 0))
    return pl.pallas_call(
        mend_kernel,
        grid=(m, 2),
        in_specs=[smem(), block, halo, halo],
        out_specs=block,
        out_shape=jax.ShapeDtypeStruct(value.shape, f32),
        input_output_aliases={1: 0},
        compiler_params=params_of(32),
        cost_estimate=pl.CostEstimate(
            flops=m * f * nz * 4 * cols, bytes_accessed=m * f * nz * 32 * cols * 4, transcendentals=0
        ),
    )(coefs, value, before, after)


def gram_kernel(n, ppd, ysp, idx_ref, coef_ref, *refs):
    ins, own_ref, other_ref, fibre, folded = refs
    me, core = idx_ref[0], idx_ref[1]
    yb = ins.shape[2]
    members = fibre.shape[0]
    rows = fibre.shape[1] // n
    half = n * rows // 2
    groups = half // (8 * n)
    edge = members * ppd * rows
    for b in range(n):
        for m in range(members):
            for j in range(ppd):
                at = (m * ppd + j) * rows
                fibre[m, b * rows : (b + 1) * rows, j * yb : j * yb + yb] = ins[b, at : at + rows, :]
    for m in range(members):
        for j in range(ppd):
            a = coef_ref[m, (me * ppd + j) // (ysp * ZS), 0]
            at = edge + 2 * (m * ppd + j)
            here = slice(j * yb, j * yb + yb)
            for b in range(n - 1):
                low, up = (b + 1) * rows - 1, (b + 1) * rows
                fibre[m, low : low + 1, here] += a * ins[b + 1, at : at + 1, :]
                fibre[m, up : up + 1, here] += a * ins[b, at + 1 : at + 2, :]
    r = lax.broadcasted_iota(jnp.int32, (half, half), 0)
    c = lax.broadcasted_iota(jnp.int32, (half, half), 1)
    contract = (((1,), (1,)), ((), ()))
    for m in range(members):
        upper = fibre[m, :half, :]
        lower = fibre[m, half:, :]
        dot = functools.partial(
            lax.dot_general, dimension_numbers=contract, precision=highest, preferred_element_type=f32
        )
        cross = dot(upper, lower)
        first = dot(upper, upper)
        second = dot(lower, lower)
        packed = jnp.where(r <= c, first, second)
        diagonal = jnp.sum(jnp.where(r == c, second, 0.0), axis=0, keepdims=True)
        for d in range(n):
            for g in range(groups):
                at = (d * groups + g) * 8
                lo = g * 2 * half
                folded[m, d, :, lo : lo + half] = cross[at : at + 8, :]
                folded[m, d, :, lo + half : lo + 2 * half] = packed[at : at + 8, :]
            tile = (d * (half // 128)) // n
            folded[m, d, :, groups * 2 * half :] = jnp.broadcast_to(
                diagonal[:, tile * 128 : tile * 128 + 128], (8, 128)
            )
    own_ref[...] = folded[core]
    other_ref[...] = folded[1 - core]


def gram(idx, coefs, pieces, members, ppd, ysp):
    n, length, yb = pieces.shape
    rows = (length - 8) // (members * ppd)
    half = n * rows // 2
    wide = half // (8 * n) * 2 * half + 128
    chunk = jax.ShapeDtypeStruct((n, 8, wide), f32)
    fibre = jax.ShapeDtypeStruct((members, n * rows, ppd * yb), f32)
    return pl.pallas_call(
        functools.partial(gram_kernel, n, ppd, ysp),
        in_specs=[smem(), smem(), vmem()],
        out_specs=[vmem()] * 3,
        out_shape=[chunk, chunk, fibre],
        scratch_shapes=[pltpu.VMEM((members, n, 8, wide), f32)],
        compiler_params=params_of(40),
    )(idx, coefs, pieces)


def spread_kernel(n, idx_ref, own_ref, got_ref, *outs):
    for k in range(n):
        at = idx_ref[0] ^ k
        outs[k][...] = own_ref[at] + got_ref[at]


def spread(idx, own, got):
    n = own.shape[0]
    return pl.pallas_call(
        functools.partial(spread_kernel, n),
        in_specs=[smem(), vmem(), vmem()],
        out_specs=[vmem()] * n,
        out_shape=[jax.ShapeDtypeStruct(own.shape[1:], f32)] * n,
        compiler_params=params_of(16),
    )(idx, own, got)


def total_kernel(*refs):
    value = refs[0][...]
    for ref in refs[1:-1]:
        value = value + ref[...]
    refs[-1][...] = value


def total(pieces):
    return pl.pallas_call(
        total_kernel,
        in_specs=[vmem()] * len(pieces),
        out_specs=vmem(),
        out_shape=jax.ShapeDtypeStruct(pieces[0].shape, f32),
        compiler_params=params_of(16),
    )(*pieces)


def inverse_factor(cov):
    size = cov.shape[0]
    shape = (8, 2 * size)
    r = lax.broadcasted_iota(jnp.int32, (size, size), 0)
    c = lax.broadcasted_iota(jnp.int32, (size, size), 1)
    both = jnp.concatenate([cov, (r == c).astype(f32)], axis=1)
    groups = [both[g : g + 8, :] for g in range(0, size, 8)]
    sub = lax.broadcasted_iota(jnp.int32, shape, 0)

    def column(value, at):
        return jnp.broadcast_to(value[:, at : at + 1], shape)

    def row(value, at):
        return jnp.broadcast_to(value[at : at + 1, :], shape)

    for g in range(size // 8):
        block = groups[g]
        columns = [column(block, 8 * g + q) for q in range(8)]
        entry = [[row(columns[q], i) for q in range(i + 1)] for i in range(8)]
        scale = []
        for q in range(8):
            scale.append(lax.rsqrt(entry[q][q]))
            for i in range(q + 1, 8):
                entry[i][q] = entry[i][q] * scale[q]
            for i in range(q + 1, 8):
                for p in range(q + 1, i + 1):
                    entry[i][p] = entry[i][p] - entry[i][q] * entry[p][q]

        def solved(raw):
            done = []
            for i in range(8):
                value = raw[i]
                for q in range(i):
                    value = value - entry[i][q] * done[q]
                done.append(value * scale[i])
            return done

        rows = solved([row(block, i) for i in range(8)])
        for h in range(g + 1, size // 8):
            below = solved([column(groups[h], 8 * g + q) for q in range(8)])
            for q in range(8):
                groups[h] = groups[h] - below[q] * rows[q]
        final = rows[0]
        for i in range(1, 8):
            final = jnp.where(sub == i, rows[i], final)
        groups[g] = final
    return jnp.concatenate([v[:, size:] for v in groups], axis=0)


def iterate_kernel(n, idx_ref, start_ref, *refs):
    ins, out_ref, folded, tails = refs[:n], refs[n], refs[n + 1], refs[n + 2]
    me, core = idx_ref[0], idx_ref[1]
    half = folded.shape[0]
    groups = half // (8 * n)
    for k in range(n):
        at = me ^ k
        for g in range(groups):
            place = pl.multiple_of(at * (8 * groups), 8) + 8 * g
            folded[pl.ds(place, 8), :] = ins[k][:, g * 2 * half : (g + 1) * 2 * half]
        tails[at] = ins[k][:, groups * 2 * half :]
    tiles = half // 128
    diagonal = jnp.concatenate([tails[t * n // tiles][0:1, :] for t in range(tiles)], axis=1)
    r = lax.broadcasted_iota(jnp.int32, (half, half), 0)
    c = lax.broadcasted_iota(jnp.int32, (half, half), 1)
    cross = folded[:, :half]
    packed = folded[:, half:]
    turned = packed.T
    first = jnp.where(r <= c, packed, turned)
    second = jnp.where(r > c, packed, jnp.where(r < c, turned, diagonal))
    matrix = split3(
        jnp.concatenate(
            [jnp.concatenate([first, cross], axis=1), jnp.concatenate([cross.T, second], axis=1)], axis=0
        )
    )
    basis = start_ref[core]
    for _ in range(ITERS):
        image = split3(apply3(split3(basis), matrix))
        basis = apply3(split3(inverse_factor(square3(image))), image)
    out_ref[...] = basis


def iterate(idx, start, pieces):
    n = len(pieces)
    _, rank, size = start.shape
    half = size // 2
    return pl.pallas_call(
        functools.partial(iterate_kernel, n),
        in_specs=[smem()] + [vmem()] * (n + 1),
        out_specs=vmem(),
        out_shape=jax.ShapeDtypeStruct((rank, size), f32),
        scratch_shapes=[pltpu.VMEM((half, 2 * half), f32), pltpu.VMEM((n, 8, 128), f32)],
        compiler_params=params_of(40),
    )(idx, start, *pieces)


def project_kernel(n, idx_ref, own_ref, got_ref, fibre, basis_ref, out_ref):
    core = idx_ref[1]
    share = out_ref.shape[2]
    basis_ref[core] = own_ref[...]
    basis_ref[1 - core] = got_ref[...]
    for m in range(fibre.shape[0]):
        value = apply3(split3(basis_ref[m]), split3(fibre[m]))
        for d in range(n):
            out_ref[d, m] = value[d * share : (d + 1) * share, :]


def project(idx, own, got, fibre, n):
    members, _, depth = fibre.shape
    rank, size = own.shape
    return pl.pallas_call(
        functools.partial(project_kernel, n),
        in_specs=[smem()] + [vmem()] * 3,
        out_specs=[vmem()] * 2,
        out_shape=[
            jax.ShapeDtypeStruct((members, rank, size), f32),
            jax.ShapeDtypeStruct((n, members, rank // n, depth), f32),
        ],
        compiler_params=params_of(32),
    )(idx, own, got, fibre)


def gather_kernel(ppd, yb, held, out):
    members, share, nf, planes, cols = out.shape
    ysp = cols // yb
    for m in range(members):
        for s in range(share):
            for p in range(nf * planes):
                f, z = divmod(p, planes)
                for h in range(ysp):
                    d, j = divmod(p * ysp + h, ppd)
                    out[m, s, f, z : z + 1, h * yb : (h + 1) * yb] = held[
                        d, m, s : s + 1, j * yb : (j + 1) * yb
                    ]


def gather(pieces, shape, ppd, yb):
    return pl.pallas_call(
        functools.partial(gather_kernel, ppd, yb),
        in_specs=[vmem()],
        out_specs=vmem(),
        out_shape=jax.ShapeDtypeStruct(shape, f32),
        compiler_params=params_of(16),
    )(pieces)


def member_params(member_index, member_table):
    table_rows = member_table.shape[0]
    onehot = (member_index[:, None] == jnp.arange(table_rows, dtype=jnp.int32)[None, :]).astype(f32)
    return jnp.einsum("mp,pfk->mfk", onehot, member_table, precision=highest)


def exchange(pieces):
    n = lax.axis_size("gx")
    return [pieces[0]] + [
        lax.ppermute(pieces[k], "gx", [(i, i ^ k) for i in range(n)]) for k in range(1, n)
    ]


def swap_cores(value):
    return lax.ppermute(value, "gy", [(0, 1), (1, 0)])


def per_device(fields, member_index, member_table, seed_x, seed_y, seed_z, start_basis):
    n = lax.axis_size("gx")
    members, nf = fields.shape[:2]
    assert lax.axis_size("gy") == 2 and members == 2
    idx = jnp.stack([lax.axis_index("gx"), lax.axis_index("gy")]).astype(jnp.int32)
    params = member_params(member_index, member_table)
    kappa, mobility, gamma, strength = (params[:, :, k] for k in range(4))
    pace = time_step * mobility
    near = pace * kappa
    coefs = jnp.stack(
        [near, 1.0 - 6.0 * near + pace, pace * (1.0 - gamma), pace * gamma, source_gain * strength], axis=-1
    )
    seeds = (
        jnp.tile(seed_x.astype(f32), (1, 6))[:, None, :],
        jnp.tile(seed_y.astype(f32), (1, 6))[:, :, None],
        jnp.tile(seed_z.astype(f32), (1, 6))[:, None, :],
    )
    ppd, yb, _ = slab_pieces(n, fields)
    up = [(i, i + 1) for i in range(n - 1)]
    down = [(j, i) for i, j in up]
    slab_side = swap_cores(edges(idx, fields, ZS, members, nf))
    pieces = lax.all_to_all(slab_step(idx, coefs, fields, slab_side, seeds, n), "gx", 0, 0)
    side = swap_cores(edges(idx, fields, fields.shape[2], 1, 2))
    value, top, bottom = bulk(idx, coefs, fields, side, seeds)
    pieces, value = lax.optimization_barrier((pieces, value))
    own, other, fibre = gram(idx, coefs, pieces, members, ppd, fields.shape[4] // yb)
    parts = exchange(spread(idx, own, swap_cores(other)))
    mine = total(parts)
    grams = exchange([mine] * n)
    grams, top, bottom = lax.optimization_barrier((grams, top, bottom))
    before, after = lax.ppermute(bottom, "gx", up), lax.ppermute(top, "gx", down)
    start = jnp.swapaxes(start_basis, 1, 2)
    basis = iterate(idx, start, grams)
    bases, rows = project(idx, basis, swap_cores(basis), fibre, n)
    rows, before, after = lax.optimization_barrier((rows, before, after))
    fields_next = mend(coefs, value, before, after)
    share = start_basis.shape[2] // n
    core = gather(lax.all_to_all(rows, "gx", 0, 0), (members, share, nf, ZS, fields.shape[4]), ppd, yb)
    return (fields_next, jnp.swapaxes(bases, 1, 2), core)


def solution(mesh):
    placed = (
        P("grp", None, None, "gx", "gy"),
        P("grp"),
        P(),
        P("grp", None),
        P("grp", None),
        P("grp", None),
        P("grp", None, None),
    )
    return jax.shard_map(
        per_device,
        mesh=mesh,
        in_specs=placed,
        out_specs=(
            P("grp", None, None, "gx", "gy"),
            P("grp", None, None),
            P("grp", "gx", None, None, "gy"),
        ),
        check_vma=False,
    )
```

```python
import functools
import jax
import jax.numpy as jnp
from jax import lax
from jax.experimental import pallas as pl
from jax.experimental.pallas import tpu as pltpu
from jax.sharding import PartitionSpec as P

ZS = 4
ITERS = 3
ZB = 8

highest = lax.Precision.HIGHEST
time_step = 0.05
bump_width = 18.0
source_gain = 0.5
f32 = jnp.float32
bf16 = jnp.bfloat16
MIB = 1 << 20


def smem():
    return pl.BlockSpec(memory_space=pltpu.SMEM)


def vmem():
    return pl.BlockSpec(memory_space=pltpu.VMEM)


def params_of(limit):
    return pltpu.CompilerParams(vmem_limit_bytes=limit * MIB)


def split3(value):
    high = value.astype(bf16)
    rest = value - high.astype(f32)
    middle = rest.astype(bf16)
    low = (rest - middle.astype(f32)).astype(bf16)
    return high, middle, low


def stacked(parts):
    return jnp.concatenate(parts, axis=0)


def apply3(left, right):
    rows = left[0].shape[0]
    first = jnp.dot(stacked(left), right[0], preferred_element_type=f32)
    second = jnp.dot(stacked(left[:2]), right[1], preferred_element_type=f32)
    third = jnp.dot(left[0], right[2], preferred_element_type=f32)
    small = first[2 * rows :] + second[rows:] + third
    return first[:rows] + (first[rows : 2 * rows] + second[:rows] + small)


def square3(parts):
    rows = parts[0].shape[0]
    whole = stacked(parts)
    every = lax.dot_general(whole, whole, (((1,), (1,)), ((), ())), preferred_element_type=f32)

    def piece(i, j):
        return every[i * rows : (i + 1) * rows, j * rows : (j + 1) * rows]

    return piece(0, 0) + (piece(0, 1) + piece(1, 0) + (piece(0, 2) + piece(2, 0) + piece(1, 1)))


def edges_kernel(idx_ref, half_ref, side_ref):
    mb, fb, planes, rows = half_ref.shape[:4]
    lane = lax.broadcasted_iota(jnp.int32, (rows, 128), 1)
    offset = jnp.where(idx_ref[1] == 0, 1, 0)
    for m in range(mb):
        for f in range(fb):
            side = jnp.zeros((rows, 128), f32)
            for z in range(planes):
                turned = pltpu.roll(half_ref[m, f, z], z + offset, 1)
                side = jnp.where(lane == z, turned, side)
            side_ref[m, f] = side


def edges(idx, fields, planes, mb, fb):
    m, f, _, rows, cols = fields.shape
    tail = cols // 128 - 1
    return pl.pallas_call(
        edges_kernel,
        grid_spec=pltpu.PrefetchScalarGridSpec(
            num_scalar_prefetch=1,
            grid=(m // mb, f // fb),
            in_specs=[
                pl.BlockSpec(
                    (mb, fb, planes, rows, 128),
                    lambda i, j, s: (i, j, 0, 0, jnp.where(s[1] == 0, tail, 0)),
                ),
            ],
            out_specs=pl.BlockSpec((mb, fb, rows, 128), lambda i, j, s: (i, j, 0, 0)),
        ),
        out_shape=jax.ShapeDtypeStruct((m, f, rows, 128), f32),
        compiler_params=params_of(32),
        cost_estimate=pl.CostEstimate(
            flops=m * f * planes * rows * 256,
            bytes_accessed=m * f * planes * rows * 128 * 4,
            transcendentals=0,
        ),
    )(idx, fields)


def step_block(idx_ref, coef_ref, refs, zb, z0, m, store):
    now, before, after, yh, sx, sy, sz = refs
    nf, rows, cols = now.shape[1], now.shape[3], now.shape[4]
    tiles = cols // 128
    wide = sx.shape[-1]
    seeds = wide // 6
    x_start = idx_ref[0] * rows
    y_start = idx_ref[1] * cols
    along_x = (x_start + lax.broadcasted_iota(jnp.int32, (rows, wide), 0)).astype(f32)
    bump_x = jnp.exp(-jnp.square(along_x - sx[0]) / bump_width)
    along_y = (y_start + lax.broadcasted_iota(jnp.int32, (wide, cols), 1)).astype(f32)
    high, middle, low = split3(jnp.exp(-jnp.square(along_y - sy[0]) / bump_width))
    part = lax.broadcasted_iota(jnp.int32, (wide, cols), 0) // seeds
    right = jnp.where(
        part == 3,
        low.astype(f32),
        jnp.where((part == 1) | (part == 5), middle.astype(f32), high.astype(f32)),
    ).astype(bf16)
    group = lax.broadcasted_iota(jnp.int32, (rows, wide), 1) // seeds
    use_low = group == 4
    use_middle = (group == 2) | (group == 5)
    lane = lax.broadcasted_iota(jnp.int32, (8, 128), 1)
    row = lax.broadcasted_iota(jnp.int32, (8, cols), 0)
    is_left = lane == 0
    is_right = lane == 127
    is_top = row == 0
    is_bottom = row == 7
    at_end = idx_ref[1] == 0
    gain_left = jnp.where(at_end, 0.0, 1.0).astype(f32)
    gain_right = jnp.where(at_end, 1.0, 0.0).astype(f32)
    coefs = [[coef_ref[m, f, k] for k in range(5)] for f in range(nf)]

    def plane(z, below_of, above_of):
        along_z = (z0 + z).astype(f32) if not isinstance(z0 + z, int) else f32(z0 + z)
        bump_z = jnp.exp(-jnp.square(along_z - sz[0]) / bump_width)
        high, middle, low = split3(bump_x * bump_z)
        left = jnp.where(
            use_low, low.astype(f32), jnp.where(use_middle, middle.astype(f32), high.astype(f32))
        ).astype(bf16)
        source = jnp.dot(left, right, preferred_element_type=f32)
        shift = jnp.where(at_end, 127 - (z0 + z), 128 - (z0 + z))
        shift = jnp.where(shift == 128, 0, shift)
        for r in range(0, rows, 8):
            cells = [now[0, f, z, r : r + 8, :] for f in range(nf)]
            squared = [c * c for c in cells]
            squares = squared[0]
            for f in range(1, nf):
                squares = squares + squared[f]
            src = source[r : r + 8, :]
            for f in range(nf):
                c = cells[f]
                a, c0, c1, c2, s = coefs[f]
                if r == 0:
                    over = jnp.zeros((1, cols), f32)
                else:
                    over = now[0, f, z, r - 1 : r, :]
                if r + 8 == rows:
                    under = jnp.zeros((1, cols), f32)
                else:
                    under = now[0, f, z, r + 8 : r + 9, :]
                up = jnp.where(is_top, over, pltpu.roll(c, 1, 0))
                down = jnp.where(is_bottom, under, pltpu.roll(c, 7, 0))
                halo = pltpu.roll(yh[0, f, r : r + 8, :], shift, 1)
                parts = [c[:, 128 * t : 128 * t + 128] for t in range(tiles)]
                fwd = [pltpu.roll(p, 1, 1) for p in parts]
                bwd = [pltpu.roll(p, 127, 1) for p in parts]
                side = []
                for t in range(tiles):
                    from_left = halo * gain_left if t == 0 else fwd[t - 1]
                    from_right = halo * gain_right if t == tiles - 1 else bwd[t + 1]
                    side.append(
                        jnp.where(is_left, from_left, fwd[t])
                        + jnp.where(is_right, from_right, bwd[t])
                    )
                near = (
                    jnp.concatenate(side, axis=1)
                    + (up + down)
                    + (below_of(f, r) + above_of(f, r))
                )
                value = a * near + c * (c0 - c1 * squared[f] - c2 * squares) + s * src
                store(f, z, r, value)

    def prior(z):
        return lambda f, r: now[0, f, z - 1, r : r + 8, :]

    def later(z):
        return lambda f, r: now[0, f, z + 1, r : r + 8, :]

    plane(0, lambda f, r: before[0, f, 0, r : r + 8, :], later(0))

    def body(z, carry):
        plane(z, prior(z), later(z))
        return carry

    lax.fori_loop(1, zb - 1, body, 0, unroll=zb <= ZS)
    plane(zb - 1, prior(zb - 1), lambda f, r: after[0, f, 0, r : r + 8, :])


def bulk_kernel(idx_ref, coef_ref, *refs):
    now = refs[0]
    out, top, bottom = refs[-3:]
    nf, rows = now.shape[1], now.shape[3]
    m, t = pl.program_id(0), pl.program_id(1)
    for f in range(nf):
        for z in range(ZB):
            top[0, f, z : z + 1, :] = now[0, f, z, 0:1, :]
            bottom[0, f, z : z + 1, :] = now[0, f, z, rows - 1 : rows, :]

    def store(f, z, r, value):
        out[0, f, z, r : r + 8, :] = value

    step_block(idx_ref, coef_ref, refs[:-3], ZB, t * ZB, m, store)


def step_specs(fields, zb, wide, place):
    m, f, nz, rows, cols = fields.shape

    def at(shape, index):
        return pl.BlockSpec(shape, lambda *g: index(*place(*g), None))

    return [
        at((1, f, zb, rows, cols), lambda i, t, s: (i, 0, t, 0, 0)),
        at((1, f, 1, rows, cols), lambda i, t, s: (i, 0, jnp.maximum(t * zb - 1, 0), 0, 0)),
        at((1, f, 1, rows, cols), lambda i, t, s: (i, 0, jnp.minimum(t * zb + zb, nz - 1), 0, 0)),
        at((1, f, rows, 128), lambda i, t, s: (i, 0, 0, 0)),
        at((1, 1, wide), lambda i, t, s: (i, 0, 0)),
        at((1, wide, 1), lambda i, t, s: (i, 0, 0)),
        at((1, 1, wide), lambda i, t, s: (i, 0, 0)),
    ]


def bulk(idx, coefs, fields, side, seeds):
    m, f, nz, rows, cols = fields.shape
    wide = seeds[0].shape[-1]
    specs = step_specs(fields, ZB, wide, lambda i, t, s: (i, t))
    return pl.pallas_call(
        bulk_kernel,
        grid_spec=pltpu.PrefetchScalarGridSpec(
            num_scalar_prefetch=1,
            grid=(m, nz // ZB),
            in_specs=[smem()] + specs,
            out_specs=[
                pl.BlockSpec((1, f, ZB, rows, cols), lambda i, t, s: (i, 0, t, 0, 0)),
                pl.BlockSpec((1, f, ZB, cols), lambda i, t, s: (i, 0, t, 0)),
                pl.BlockSpec((1, f, ZB, cols), lambda i, t, s: (i, 0, t, 0)),
            ],
        ),
        out_shape=[
            jax.ShapeDtypeStruct(fields.shape, f32),
            jax.ShapeDtypeStruct((m, f, nz, cols), f32),
            jax.ShapeDtypeStruct((m, f, nz, cols), f32),
        ],
        compiler_params=params_of(40),
        cost_estimate=pl.CostEstimate(
            flops=fields.size * 30, bytes_accessed=fields.size * 10, transcendentals=0
        ),
    )(idx, coefs, fields, fields, fields, side, *seeds)


def slab_kernel(n, ppd, yb, idx_ref, coef_ref, *refs):
    ins, out = refs[:7], refs[7]
    now = ins[0]
    nf, rows = now.shape[1], now.shape[3]
    m = pl.program_id(0)
    ysp = now.shape[4] // yb
    members = (out.shape[1] - 8) // (ppd * rows)

    def store(f, z, r, value):
        for h in range(ysp):
            d, j = divmod((f * ZS + z) * ysp + h, ppd)
            at = pl.multiple_of((m * ppd + j) * rows, rows) + r
            out[d, pl.ds(at, 8), :] = value[:, h * yb : h * yb + yb]

    step_block(idx_ref, coef_ref, ins, ZS, 0, m, store)
    for i in range(members):

        @pl.when(m == i)
        def _():
            for f in range(nf):
                for z in range(ZS):
                    for h in range(ysp):
                        d, j = divmod((f * ZS + z) * ysp + h, ppd)
                        at = members * ppd * rows + 2 * (i * ppd + j)
                        out[d, at : at + 1, :] = now[0, f, z, 0:1, h * yb : h * yb + yb]
                        out[d, at + 1 : at + 2, :] = now[0, f, z, rows - 1 : rows, h * yb : h * yb + yb]


def slab_pieces(n, fields):
    _, f, _, _, cols = fields.shape
    count = f * ZS
    ysp = max(1, n // count)
    return max(1, count // n), cols // ysp, count * ysp


def slab_step(idx, coefs, fields, side, seeds, n):
    m, f, nz, rows, cols = fields.shape
    wide = seeds[0].shape[-1]
    ppd, yb, pieces = slab_pieces(n, fields)
    piece = jax.ShapeDtypeStruct((n, m * ppd * rows + 8, yb), f32)
    specs = step_specs(fields, ZS, wide, lambda i, t, s: (i, t))
    return pl.pallas_call(
        functools.partial(slab_kernel, n, ppd, yb),
        grid_spec=pltpu.PrefetchScalarGridSpec(
            num_scalar_prefetch=1,
            grid=(m, 1),
            in_specs=[smem()] + specs,
            out_specs=pl.BlockSpec(piece.shape, lambda i, t, s: (0, 0, 0)),
        ),
        out_shape=piece,
        compiler_params=params_of(32),
        cost_estimate=pl.CostEstimate(
            flops=m * f * ZS * rows * cols * 30,
            bytes_accessed=m * f * ZS * rows * cols * 10,
            transcendentals=0,
        ),
    )(idx, coefs, fields, fields, fields, side, *seeds)


def mend_kernel(coef_ref, value_ref, before_ref, after_ref, out_ref):
    m, end = pl.program_id(0), pl.program_id(1)
    nf, planes = out_ref.shape[1:3]
    out_ref[...] = value_ref[...]

    @pl.when(end == 0)
    def _():
        for f in range(nf):
            a = coef_ref[m, f, 0]
            for z in range(planes):
                out_ref[0, f, z, 0:1, :] = value_ref[0, f, z, 0:1, :] + a * before_ref[0, f, z : z + 1, :]

    @pl.when(end == 1)
    def _():
        for f in range(nf):
            a = coef_ref[m, f, 0]
            for z in range(planes):
                out_ref[0, f, z, 7:8, :] = value_ref[0, f, z, 7:8, :] + a * after_ref[0, f, z : z + 1, :]


def mend(coefs, value, before, after):
    m, f, nz, rows, cols = value.shape
    last = rows // 8 - 1
    block = pl.BlockSpec((1, f, nz, 8, cols), lambda i, e: (i, 0, 0, e * last, 0))
    halo = pl.BlockSpec((1, f, nz, cols), lambda i, e: (i, 0, 0, 0))
    return pl.pallas_call(
        mend_kernel,
        grid=(m, 2),
        in_specs=[smem(), block, halo, halo],
        out_specs=block,
        out_shape=jax.ShapeDtypeStruct(value.shape, f32),
        input_output_aliases={1: 0},
        compiler_params=params_of(32),
        cost_estimate=pl.CostEstimate(
            flops=m * f * nz * 4 * cols, bytes_accessed=m * f * nz * 32 * cols * 4, transcendentals=0
        ),
    )(coefs, value, before, after)


def gram_kernel(n, ppd, ysp, idx_ref, coef_ref, *refs):
    ins, own_ref, other_ref, fibre, folded = refs
    me, core = idx_ref[0], idx_ref[1]
    yb = ins.shape[2]
    members = fibre.shape[0]
    rows = fibre.shape[1] // n
    half = n * rows // 2
    groups = half // (8 * n)
    edge = members * ppd * rows
    for b in range(n):
        for m in range(members):
            for j in range(ppd):
                at = (m * ppd + j) * rows
                fibre[m, b * rows : (b + 1) * rows, j * yb : j * yb + yb] = ins[b, at : at + rows, :]
    for m in range(members):
        for j in range(ppd):
            a = coef_ref[m, (me * ppd + j) // (ysp * ZS), 0]
            at = edge + 2 * (m * ppd + j)
            here = slice(j * yb, j * yb + yb)
            for b in range(n - 1):
                low, up = (b + 1) * rows - 1, (b + 1) * rows
                fibre[m, low : low + 1, here] += a * ins[b + 1, at : at + 1, :]
                fibre[m, up : up + 1, here] += a * ins[b, at + 1 : at + 2, :]
    r = lax.broadcasted_iota(jnp.int32, (half, half), 0)
    c = lax.broadcasted_iota(jnp.int32, (half, half), 1)
    contract = (((1,), (1,)), ((), ()))
    for m in range(members):
        upper = fibre[m, :half, :]
        lower = fibre[m, half:, :]
        dot = functools.partial(
            lax.dot_general, dimension_numbers=contract, precision=highest, preferred_element_type=f32
        )
        cross = dot(upper, lower)
        first = dot(upper, upper)
        second = dot(lower, lower)
        packed = jnp.where(r <= c, first, second)
        diagonal = jnp.sum(jnp.where(r == c, second, 0.0), axis=0, keepdims=True)
        for d in range(n):
            for g in range(groups):
                at = (d * groups + g) * 8
                lo = g * 2 * half
                folded[m, d, :, lo : lo + half] = cross[at : at + 8, :]
                folded[m, d, :, lo + half : lo + 2 * half] = packed[at : at + 8, :]
            tile = (d * (half // 128)) // n
            folded[m, d, :, groups * 2 * half :] = jnp.broadcast_to(
                diagonal[:, tile * 128 : tile * 128 + 128], (8, 128)
            )
    own_ref[...] = folded[core]
    other_ref[...] = folded[1 - core]


def gram(idx, coefs, pieces, members, ppd, ysp):
    n, length, yb = pieces.shape
    rows = (length - 8) // (members * ppd)
    half = n * rows // 2
    wide = half // (8 * n) * 2 * half + 128
    chunk = jax.ShapeDtypeStruct((n, 8, wide), f32)
    fibre = jax.ShapeDtypeStruct((members, n * rows, ppd * yb), f32)
    return pl.pallas_call(
        functools.partial(gram_kernel, n, ppd, ysp),
        in_specs=[smem(), smem(), vmem()],
        out_specs=[vmem()] * 3,
        out_shape=[chunk, chunk, fibre],
        scratch_shapes=[pltpu.VMEM((members, n, 8, wide), f32)],
        compiler_params=params_of(40),
    )(idx, coefs, pieces)


def spread_kernel(n, idx_ref, own_ref, got_ref, *outs):
    for k in range(n):
        at = idx_ref[0] ^ k
        outs[k][...] = own_ref[at] + got_ref[at]


def spread(idx, own, got):
    n = own.shape[0]
    return pl.pallas_call(
        functools.partial(spread_kernel, n),
        in_specs=[smem(), vmem(), vmem()],
        out_specs=[vmem()] * n,
        out_shape=[jax.ShapeDtypeStruct(own.shape[1:], f32)] * n,
        compiler_params=params_of(16),
    )(idx, own, got)


def total_kernel(*refs):
    value = refs[0][...]
    for ref in refs[1:-1]:
        value = value + ref[...]
    refs[-1][...] = value


def total(pieces):
    return pl.pallas_call(
        total_kernel,
        in_specs=[vmem()] * len(pieces),
        out_specs=vmem(),
        out_shape=jax.ShapeDtypeStruct(pieces[0].shape, f32),
        compiler_params=params_of(16),
    )(*pieces)


def inverse_factor(cov):
    size = cov.shape[0]
    shape = (8, 2 * size)
    r = lax.broadcasted_iota(jnp.int32, (size, size), 0)
    c = lax.broadcasted_iota(jnp.int32, (size, size), 1)
    both = jnp.concatenate([cov, (r == c).astype(f32)], axis=1)
    groups = [both[g : g + 8, :] for g in range(0, size, 8)]
    sub = lax.broadcasted_iota(jnp.int32, shape, 0)

    def column(value, at):
        return jnp.broadcast_to(value[:, at : at + 1], shape)

    def row(value, at):
        return jnp.broadcast_to(value[at : at + 1, :], shape)

    for g in range(size // 8):
        block = groups[g]
        columns = [column(block, 8 * g + q) for q in range(8)]
        entry = [[row(columns[q], i) for q in range(i + 1)] for i in range(8)]
        scale = []
        for q in range(8):
            scale.append(lax.rsqrt(entry[q][q]))
            for i in range(q + 1, 8):
                entry[i][q] = entry[i][q] * scale[q]
            for i in range(q + 1, 8):
                for p in range(q + 1, i + 1):
                    entry[i][p] = entry[i][p] - entry[i][q] * entry[p][q]

        def solved(raw):
            done = []
            for i in range(8):
                value = raw[i]
                for q in range(i):
                    value = value - entry[i][q] * done[q]
                done.append(value * scale[i])
            return done

        rows = solved([row(block, i) for i in range(8)])
        for h in range(g + 1, size // 8):
            below = solved([column(groups[h], 8 * g + q) for q in range(8)])
            for q in range(8):
                groups[h] = groups[h] - below[q] * rows[q]
        final = rows[0]
        for i in range(1, 8):
            final = jnp.where(sub == i, rows[i], final)
        groups[g] = final
    return jnp.concatenate([v[:, size:] for v in groups], axis=0)


def iterate_kernel(n, idx_ref, start_ref, *refs):
    ins, out_ref, folded, tails = refs[:n], refs[n], refs[n + 1], refs[n + 2]
    me, core = idx_ref[0], idx_ref[1]
    half = folded.shape[0]
    groups = half // (8 * n)
    for k in range(n):
        at = me ^ k
        for g in range(groups):
            place = pl.multiple_of(at * (8 * groups), 8) + 8 * g
            folded[pl.ds(place, 8), :] = ins[k][:, g * 2 * half : (g + 1) * 2 * half]
        tails[at] = ins[k][:, groups * 2 * half :]
    tiles = half // 128
    diagonal = jnp.concatenate([tails[t * n // tiles][0:1, :] for t in range(tiles)], axis=1)
    r = lax.broadcasted_iota(jnp.int32, (half, half), 0)
    c = lax.broadcasted_iota(jnp.int32, (half, half), 1)
    cross = folded[:, :half]
    packed = folded[:, half:]
    turned = packed.T
    first = jnp.where(r <= c, packed, turned)
    second = jnp.where(r > c, packed, jnp.where(r < c, turned, diagonal))
    matrix = split3(
        jnp.concatenate(
            [jnp.concatenate([first, cross], axis=1), jnp.concatenate([cross.T, second], axis=1)], axis=0
        )
    )
    basis = start_ref[core]
    for _ in range(ITERS):
        image = split3(apply3(split3(basis), matrix))
        basis = apply3(split3(inverse_factor(square3(image))), image)
    out_ref[...] = basis


def iterate(idx, start, pieces):
    n = len(pieces)
    _, rank, size = start.shape
    half = size // 2
    return pl.pallas_call(
        functools.partial(iterate_kernel, n),
        in_specs=[smem()] + [vmem()] * (n + 1),
        out_specs=vmem(),
        out_shape=jax.ShapeDtypeStruct((rank, size), f32),
        scratch_shapes=[pltpu.VMEM((half, 2 * half), f32), pltpu.VMEM((n, 8, 128), f32)],
        compiler_params=params_of(40),
    )(idx, start, *pieces)


def project_kernel(n, idx_ref, own_ref, got_ref, fibre, basis_ref, out_ref):
    core = idx_ref[1]
    share = out_ref.shape[2]
    basis_ref[core] = own_ref[...]
    basis_ref[1 - core] = got_ref[...]
    for m in range(fibre.shape[0]):
        value = apply3(split3(basis_ref[m]), split3(fibre[m]))
        for d in range(n):
            out_ref[d, m] = value[d * share : (d + 1) * share, :]


def project(idx, own, got, fibre, n):
    members, _, depth = fibre.shape
    rank, size = own.shape
    return pl.pallas_call(
        functools.partial(project_kernel, n),
        in_specs=[smem()] + [vmem()] * 3,
        out_specs=[vmem()] * 2,
        out_shape=[
            jax.ShapeDtypeStruct((members, rank, size), f32),
            jax.ShapeDtypeStruct((n, members, rank // n, depth), f32),
        ],
        compiler_params=params_of(32),
    )(idx, own, got, fibre)


def gather_kernel(ppd, yb, held, out):
    members, share, nf, planes, cols = out.shape
    ysp = cols // yb
    for m in range(members):
        for s in range(share):
            for p in range(nf * planes):
                f, z = divmod(p, planes)
                for h in range(ysp):
                    d, j = divmod(p * ysp + h, ppd)
                    out[m, s, f, z : z + 1, h * yb : (h + 1) * yb] = held[
                        d, m, s : s + 1, j * yb : (j + 1) * yb
                    ]


def gather(pieces, shape, ppd, yb):
    return pl.pallas_call(
        functools.partial(gather_kernel, ppd, yb),
        in_specs=[vmem()],
        out_specs=vmem(),
        out_shape=jax.ShapeDtypeStruct(shape, f32),
        compiler_params=params_of(16),
    )(pieces)


def member_params(member_index, member_table):
    table_rows = member_table.shape[0]
    onehot = (member_index[:, None] == jnp.arange(table_rows, dtype=jnp.int32)[None, :]).astype(f32)
    return jnp.einsum("mp,pfk->mfk", onehot, member_table, precision=highest)


def exchange(pieces):
    n = lax.axis_size("gx")
    return [pieces[0]] + [
        lax.ppermute(pieces[k], "gx", [(i, i ^ k) for i in range(n)]) for k in range(1, n)
    ]


def swap_cores(value):
    return lax.ppermute(value, "gy", [(0, 1), (1, 0)])


def per_device(fields, member_index, member_table, seed_x, seed_y, seed_z, start_basis):
    n = lax.axis_size("gx")
    members, nf = fields.shape[:2]
    assert lax.axis_size("gy") == 2 and members == 2
    idx = jnp.stack([lax.axis_index("gx"), lax.axis_index("gy")]).astype(jnp.int32)
    params = member_params(member_index, member_table)
    kappa, mobility, gamma, strength = (params[:, :, k] for k in range(4))
    pace = time_step * mobility
    near = pace * kappa
    coefs = jnp.stack(
        [near, 1.0 - 6.0 * near + pace, pace * (1.0 - gamma), pace * gamma, source_gain * strength], axis=-1
    )
    seeds = (
        jnp.tile(seed_x.astype(f32), (1, 6))[:, None, :],
        jnp.tile(seed_y.astype(f32), (1, 6))[:, :, None],
        jnp.tile(seed_z.astype(f32), (1, 6))[:, None, :],
    )
    ppd, yb, _ = slab_pieces(n, fields)
    up = [(i, i + 1) for i in range(n - 1)]
    down = [(j, i) for i, j in up]
    slab_side = swap_cores(edges(idx, fields, ZS, members, nf))
    pieces = lax.all_to_all(slab_step(idx, coefs, fields, slab_side, seeds, n), "gx", 0, 0)
    side = swap_cores(edges(idx, fields, fields.shape[2], 1, 2))
    value, top, bottom = bulk(idx, coefs, fields, side, seeds)
    pieces, value = lax.optimization_barrier((pieces, value))
    own, other, fibre = gram(idx, coefs, pieces, members, ppd, fields.shape[4] // yb)
    parts = exchange(spread(idx, own, swap_cores(other)))
    mine = total(parts)
    grams = exchange([mine] * n)
    grams, top, bottom = lax.optimization_barrier((grams, top, bottom))
    before, after = lax.ppermute(bottom, "gx", up), lax.ppermute(top, "gx", down)
    start = jnp.swapaxes(start_basis, 1, 2)
    basis = iterate(idx, start, grams)
    bases, rows = project(idx, basis, swap_cores(basis), fibre, n)
    rows, before, after = lax.optimization_barrier((rows, before, after))
    fields_next = mend(coefs, value, before, after)
    share = start_basis.shape[2] // n
    core = gather(lax.all_to_all(rows, "gx", 0, 0), (members, share, nf, ZS, fields.shape[4]), ppd, yb)
    return (fields_next, jnp.swapaxes(bases, 1, 2), core)


def solution(mesh):
    placed = (
        P("grp", None, None, "gx", "gy"),
        P("grp"),
        P(),
        P("grp", None),
        P("grp", None),
        P("grp", None),
        P("grp", None, None),
    )
    return jax.shard_map(
        per_device,
        mesh=mesh,
        in_specs=placed,
        out_specs=(
            P("grp", None, None, "gx", "gy"),
            P("grp", None, None),
            P("grp", "gx", None, None, "gy"),
        ),
        check_vma=False,
    )
```
